256 devices in a mesh: grp: 2 (over core), gx: 32 (over z, x), gy: 4 (over y).
Axes of the slice: x: 4, y: 4, z: 8, core: 2. Of those that a mesh axis runs over, the one named last changes fastest.
Arguments:
- section_levels: bfloat16 [2, 10, 1024, 128, 128], P('grp', None, 'gx', 'gy'), may hold values from -6 to 6
- to_cells: bfloat16 [256, 32, 4, 16], P('gx', 'gy'), may hold values from -1.5 to 1.5
- to_nodes: bfloat16 [256, 32, 16, 4], P('gx', 'gy'), may hold values from -3 to 3
- owner_map: int32 [32, 4, 64, 1], P('gx', 'gy'), may hold values from 0 to 127; in each aligned block of 64 rows (0 to 63, 64 to 127, ..., all dimensions but the last counted through in order) at most 2 rows name the same one
- forcing: float32 [32, 4, 8, 4, 256], P('gx', 'gy'), may hold values from -6 to 6
- vertical_map: float32 [128, 128], replicated, may hold values from -0.5 to 0.5
- coupling: float32 [8, 10], replicated, may hold values from -2 to 2
- relaxation: float32 [8, 128], replicated, may hold values from 0.2 to 2
Outputs:
- new_state: bfloat16 [10, 1024, 128, 128], P(None, 'gx', 'gy', 'grp')
The draws below stay inside these ranges and needn't reach their ends.
Inputs may be any that keep to these rules, and one draw needn't show every extreme that they name: `owner_map`: no physics owner receives more than 2 elements from the elements of one device, and some owner receives exactly 2 from some device.
All inputs are finite; a program needn't handle non-finite values.
Results may differ from the reference program's by a relative error of at most 0.0051.
Values may be sent and summed in bfloat16 or wider, within the bound.
A program may use at most 128 MiB of HBM per device.

```python
import math
import jax
import jax.numpy as jnp
import numpy as np
from jax import lax

LEV = 128
NF = 10
NTEND = 8
EX_DEV = 8
EY_DEV = 8
CAP = 2
SLOTS = 256
NEX = 256
NEY = 32
NX = 1024
NY = 128
N_GX = 32
N_GY = 4


def shard_levels(own_key, dims, shards, least, high):
    loudness, own = 1.0, jax.random.fold_in(own_key, 6)
    for dim, blocks in shards:
        steps = jnp.exp(jax.random.uniform(jax.random.fold_in(own, dim), (blocks,), jnp.float32, least / len(shards), high / len(shards)))
        loudness = loudness * jnp.repeat(steps, dims[dim] // blocks).reshape([-1 if axis == dim else 1 for axis in range(len(dims))])
    return loudness


def routed_block(own_key, own, number, rows, amount, top, limit, lean):
    sequence = jax.random.permutation(own_key, amount)
    packed, usual = load_shares(amount, rows * top, limit, lean, True), load_shares(amount, rows * top, limit, lean, False)
    places = jnp.arange(amount)

    def named(lengths, offset_by):
        used = int((lengths > 0).sum())
        fixed = max(1, used // 4)
        moved = fixed + (places - fixed + offset_by * (used - fixed)) % max(1, amount - fixed)
        return jnp.zeros((amount,), jnp.int32).at[sequence[jnp.where(places < fixed, places, moved)]].set(jnp.asarray(lengths, jnp.int32))

    lengths = jnp.where(number % 4 == 0, named(packed, number // 4), named(usual, number - number // 4 - 1))
    mixed = jax.random.permutation(jax.random.fold_in(own, 3), amount)
    donor, receiver = mixed[0:amount // 2 * 2:2], mixed[1:amount // 2 * 2:2]
    room = jnp.minimum(lengths[donor] - 1, limit - lengths[receiver]) // 2
    room = jnp.where((donor == sequence[0]) | (receiver == sequence[0]) | (lengths[receiver] == 0), 0, jnp.maximum(room, 0))
    moved = jax.random.randint(jax.random.fold_in(own, 4), (amount // 2,), 0, 1 << 20) % (room + 1)
    lengths = lengths.at[donor].add(-moved).at[receiver].add(moved)
    labels = jnp.searchsorted(jnp.cumsum(lengths), jnp.arange(rows * top), side="right").astype(jnp.int32)
    table = labels.reshape(top, rows).T
    table = table[jax.random.permutation(jax.random.fold_in(own, 1), rows)]
    offset_by = jax.random.randint(jax.random.fold_in(own, 2), (rows, 1), 0, top)
    return jnp.take_along_axis(table, (jnp.arange(top)[None, :] + offset_by) % top, axis=1)


def load_shares(amount, total, limit, skew, full):
    weights = [(1 << 20) // math.isqrt(grade ** skew) + 1 for grade in range(1, amount + 1)]
    largest = limit if full else min(limit, max(-(-total // amount), total * weights[0] // sum(weights)))
    least = 1 if total - largest >= amount - 1 else 0
    given, surplus = [largest] + [least] * (amount - 1), total - largest - least * (amount - 1)
    while surplus > 0:
        free = [i for i in range(1, amount) if given[i] < largest] or [i for i in range(1, amount) if given[i] < limit]
        pool, budget = sum([weights[i] for i in free]), surplus
        for i in free:
            extra = min(limit - given[i], max(1, budget * weights[i] // pool), surplus)
            given[i] = given[i] + extra
            surplus = surplus - extra
    return np.array(given)


def centred(own_key, dims, width, most, pieces=(), kind=jnp.bfloat16):
    factor_of = shard_levels(own_key, dims, pieces, -0.22, 0.18) if pieces else 1.0
    result = jax.random.normal(own_key, dims, jnp.float32) * width * factor_of
    return jnp.minimum(jnp.maximum(result, -most), most).astype(kind)


def setup_inputs(seed: int = 0) -> dict:
    key_of = jax.random.split(jax.random.key(seed), 9)
    section_levels = centred(key_of[0], (2, NF, NX, NY, LEV), 1.0, 6.0, ((0, 2), (2, 32), (3, 4)))
    to_cells = centred(key_of[1], (NEX, NEY, 4, 16), 16 ** -0.5, 1.5, ((0, 32), (1, 4)))
    to_nodes = centred(key_of[2], (NEX, NEY, 16, 4), 4 ** -0.5, 3.0, ((0, 32), (1, 4)))
    owner_map_keys = jax.random.split(jax.random.fold_in(key_of[3], 1), N_GX * N_GY * (EX_DEV * EY_DEV) // (EX_DEV * EY_DEV))
    owner_map_turns = jax.random.permutation(jax.random.fold_in(key_of[3], 3), N_GX * N_GY * (EX_DEV * EY_DEV) // (EX_DEV * EY_DEV))
    owner_map = jax.vmap(lambda own, number: routed_block(jax.random.fold_in(key_of[3], 2), own, number, EX_DEV * EY_DEV, N_GX * N_GY, 1, CAP, 2))(owner_map_keys, owner_map_turns).reshape((N_GX, N_GY, EX_DEV * EY_DEV, 1))
    forcing = centred(key_of[4], (N_GX, N_GY, NTEND, 4, SLOTS), 1.0, 6.0, ((0, 32), (1, 4)), jnp.float32)
    vertical_map = centred(key_of[5], (LEV, LEV), LEV ** -0.5, 0.5, (), jnp.float32)
    coupling = centred(key_of[6], (NTEND, NF), NF ** -0.5, 2.0, (), jnp.float32)
    relaxation = jnp.clip(jnp.exp(jax.random.uniform(key_of[7], (NTEND, LEV), jnp.float32, math.log(0.2), math.log(2.0))), 0.2, 2.0)
    return {"section_levels": section_levels, "to_cells": to_cells, "to_nodes": to_nodes, "owner_map": owner_map, "forcing": forcing, "vertical_map": vertical_map, "coupling": coupling, "relaxation": relaxation}


dt_dynamics = 0.1
dt_physics = 0.25
highest = lax.Precision.HIGHEST

def gll_derivative():
    points = np.array([-1.0, -1.0 / np.sqrt(5.0), 1.0 / np.sqrt(5.0), 1.0])
    barycentric = np.ones(4)
    for first in range(4):
        for second in range(4):
            if first != second:
                barycentric[first] = barycentric[first] / (points[first] - points[second])
    matrix = np.zeros((4, 4))
    for first in range(4):
        for second in range(4):
            if first != second:
                matrix[first, second] = barycentric[second] / barycentric[first] / (points[first] - points[second])
        matrix[first, first] = -np.sum(matrix[first])
    return jnp.asarray(matrix, jnp.float32)

def derivatives(field):
    derivative = gll_derivative()
    full_shape = field.shape
    lead_dims = full_shape[:-3]
    extent_x, extent_y, levels = full_shape[-3:]
    blocks = field.reshape(lead_dims + (extent_x // 4, 4, extent_y, levels))
    along_x = jnp.einsum('ij,...ejyl->...eiyl', derivative, blocks, precision=highest).reshape(full_shape)
    blocks = field.reshape(lead_dims + (extent_x, extent_y // 4, 4, levels))
    along_y = jnp.einsum('ij,...xejl->...xeil', derivative, blocks, precision=highest).reshape(full_shape)
    return (along_x, along_y)

def edge_average(center, lower_side, upper_side, axis):
    position = lax.broadcasted_iota(jnp.int32, center.shape, axis) % 4
    upper_mean = 0.5 * (center + upper_side)
    lower_mean = 0.5 * (center + lower_side)
    return jnp.where(position == 3, upper_mean, jnp.where(position == 0, lower_mean, center))

def column_physics(cells, local_forcing, vertical_map, coupling, relaxation):
    ntend = coupling.shape[0]
    mixed = jnp.einsum('sfpl,lm->sfpm', cells, vertical_map, precision=highest)
    response = jnp.einsum('gf,sfpl->sgpl', coupling, jnp.tanh(mixed), precision=highest)
    damping = relaxation[None, :, None, :] * (cells[:, :ntend] - mixed[:, :ntend])
    tendency = response - damping + local_forcing[..., None]
    return tendency.astype(jnp.bfloat16)

def reference(section_levels, to_cells, to_nodes, owner_map, forcing, vertical_map, coupling, relaxation):
    winds_x = section_levels[0, 0].astype(jnp.float32)
    winds_y = section_levels[0, 1].astype(jnp.float32)

    def dynamics(pair_values):
        current, initial = pair_values
        field = current.astype(jnp.float32)
        along_x, along_y = derivatives(field)
        tendency = -(winds_x * along_x + winds_y * along_y)
        tendency = edge_average(tendency, jnp.roll(tendency, 1, 0), jnp.roll(tendency, -1, 0), 0)
        tendency = edge_average(tendency, jnp.roll(tendency, 1, 1), jnp.roll(tendency, -1, 1), 1)
        rounded = lax.optimization_barrier(tendency.astype(jnp.bfloat16))
        return (initial.astype(jnp.float32) + dt_dynamics * rounded.astype(jnp.float32)).astype(jnp.bfloat16)
    advanced = lax.map(dynamics, (section_levels[0], section_levels[1]))
    owners = owner_map[..., 0]
    onehot = (owners[..., None] == jnp.arange(N_GX * N_GY, dtype=jnp.int32)).astype(jnp.int32)
    earlier = jnp.cumsum(onehot, axis=2) - onehot
    rank = lax.optimization_barrier(jnp.sum(earlier * onehot, axis=3))
    sources = (jnp.arange(N_GX, dtype=jnp.int32)[:, None] * N_GY + jnp.arange(N_GY, dtype=jnp.int32)[None, :])[..., None]
    slots = (sources * CAP + rank).astype(jnp.int32)
    gathered = forcing[owners // N_GY, owners % N_GY, :, :, slots]
    element_count = EX_DEV * EY_DEV

    def physics(block):
        field = lax.dynamic_slice_in_dim(advanced, block * 4 * EX_DEV, 4 * EX_DEV, 1)
        grid = field.reshape(NF, EX_DEV, 4, N_GY, EY_DEV, 4, LEV).transpose(3, 1, 4, 0, 2, 5, 6)
        grid = grid.reshape(N_GY * element_count, NF, 16, LEV).astype(jnp.float32)
        weights_in = lax.dynamic_slice_in_dim(to_cells, block * EX_DEV, EX_DEV, 0)
        weights_in = weights_in.reshape(EX_DEV, N_GY, EY_DEV, 4, 16).transpose(1, 0, 2, 3, 4)
        weights_in = weights_in.reshape(N_GY * element_count, 4, 16).astype(jnp.float32)
        cells = jnp.einsum('epn,efnl->efpl', weights_in, grid, precision=highest)
        local_forcing = lax.dynamic_index_in_dim(gathered, block, 0, keepdims=False)
        local_forcing = local_forcing.reshape(N_GY * element_count, NTEND, 4)
        tendency = column_physics(cells, local_forcing, vertical_map, coupling, relaxation)
        weights_out = lax.dynamic_slice_in_dim(to_nodes, block * EX_DEV, EX_DEV, 0)
        weights_out = weights_out.reshape(EX_DEV, N_GY, EY_DEV, 16, 4).transpose(1, 0, 2, 3, 4)
        weights_out = weights_out.reshape(N_GY * element_count, 16, 4).astype(jnp.float32)
        nodal = jnp.einsum('enp,egpl->egnl', weights_out, tendency.astype(jnp.float32), precision=highest)
        nodal = nodal.reshape(N_GY, EX_DEV, EY_DEV, NTEND, 4, 4, LEV).transpose(3, 1, 4, 0, 2, 5, 6)
        nodal = nodal.reshape(NTEND, 4 * EX_DEV, NY, LEV)
        updated = field[:NTEND].astype(jnp.float32) + dt_physics * nodal
        return jnp.concatenate([updated.astype(jnp.bfloat16), field[NTEND:]], axis=0)
    stacked = lax.map(physics, jnp.arange(N_GX, dtype=jnp.int32))
    return stacked.transpose(1, 0, 2, 3, 4).reshape(NF, NX, NY, LEV)
```

```python
import jax
import jax.numpy as jnp
import numpy as np
from jax import lax
from jax.sharding import PartitionSpec as P

dt_dynamics = 0.1
dt_physics = 0.25
highest = lax.Precision.HIGHEST


def with_halo(cells, sides, width):
    for axis, dim in sides:
        count = lax.axis_size(axis)
        head = lax.slice_in_dim(cells, 0, width, axis=dim)
        tail = lax.slice_in_dim(cells, cells.shape[dim] - width, cells.shape[dim], axis=dim)
        cells = jnp.concatenate(
            [
                lax.ppermute(tail, axis, [(i, (i + 1) % count) for i in range(count)]),
                cells,
                lax.ppermute(head, axis, [((i + 1) % count, i) for i in range(count)]),
            ],
            axis=dim,
        )
    return cells


def from_partner(shard, axis, bit):
    return lax.ppermute(shard, axis, [(i, i ^ 1 << bit) for i in range(lax.axis_size(axis))])


def gll_derivative():
    points = np.array([-1.0, -1.0 / np.sqrt(5.0), 1.0 / np.sqrt(5.0), 1.0])
    barycentric = np.ones(4)
    for first in range(4):
        for second in range(4):
            if first != second:
                barycentric[first] = barycentric[first] / (points[first] - points[second])
    matrix = np.zeros((4, 4))
    for first in range(4):
        for second in range(4):
            if first != second:
                matrix[first, second] = (
                    barycentric[second] / barycentric[first] / (points[first] - points[second])
                )
        matrix[first, first] = -np.sum(matrix[first])
    return jnp.asarray(matrix, jnp.float32)


def derivatives(field):
    derivative = gll_derivative()
    full_shape = field.shape
    lead_dims = full_shape[:-3]
    extent_x, extent_y, levels = full_shape[-3:]
    blocks = field.reshape(lead_dims + (extent_x // 4, 4, extent_y, levels))
    along_x = jnp.einsum("ij,...ejyl->...eiyl", derivative, blocks, precision=highest).reshape(
        full_shape
    )
    blocks = field.reshape(lead_dims + (extent_x, extent_y // 4, 4, levels))
    along_y = jnp.einsum("ij,...xejl->...xeil", derivative, blocks, precision=highest).reshape(
        full_shape
    )
    return (along_x, along_y)


def edge_average(center, lower_side, upper_side, axis):
    position = lax.broadcasted_iota(jnp.int32, center.shape, axis) % 4
    upper_mean = 0.5 * (center + upper_side)
    lower_mean = 0.5 * (center + lower_side)
    return jnp.where(position == 3, upper_mean, jnp.where(position == 0, lower_mean, center))


def shards(
    section_levels, to_cells, to_nodes, owner_map, forcing, vertical_map, coupling, relaxation
):
    member = lax.axis_index("grp")
    current = section_levels[0]
    fields, extent_x, extent_y, levels = current.shape
    field = current.astype(jnp.float32)
    along_x, along_y = derivatives(field)
    tendency = -(field[0] * along_x + field[1] * along_y)
    padded = with_halo(tendency, (("gx", 1),), 1)
    tendency = edge_average(tendency, padded[:, :-2], padded[:, 2:], 1)
    padded = with_halo(tendency, (("gy", 2),), 1)
    tendency = edge_average(tendency, padded[:, :, :-2], padded[:, :, 2:], 2)
    rounded = tendency.astype(jnp.bfloat16)
    outgoing = jnp.where(member == 0, rounded, current)
    incoming = from_partner(outgoing, "grp", 0)
    initial = jnp.where(member == 0, incoming, current)
    section_rate = jnp.where(member == 0, rounded, incoming)
    advanced = (
        initial.astype(jnp.float32) + dt_dynamics * section_rate.astype(jnp.float32)
    ).astype(jnp.bfloat16)
    elems_x = to_cells.shape[0]
    elems_y = to_cells.shape[1]
    element_count = elems_x * elems_y
    peer_count = lax.axis_size(("gx", "gy"))
    owners = owner_map.reshape(element_count)
    same = owners[:, None] == owners[None, :]
    earlier = lax.broadcasted_iota(jnp.int32, same.shape, 0) > lax.broadcasted_iota(
        jnp.int32, same.shape, 1
    )
    rank = jnp.sum((same & earlier).astype(jnp.int32), axis=1)
    ntend = coupling.shape[0]
    capacity = forcing.shape[-1] // peer_count
    outgoing_forcing = forcing[0, 0].reshape(ntend * 4, peer_count, capacity).transpose(1, 2, 0)
    received = lax.all_to_all(
        outgoing_forcing, ("gx", "gy"), split_axis=0, concat_axis=0, tiled=True
    )
    received = received.reshape(peer_count * capacity, ntend * 4)
    local_forcing = jnp.take(received, owners * capacity + rank, axis=0)
    local_forcing = local_forcing.reshape(element_count, ntend, 4)
    nodes = advanced.reshape(fields, elems_x, 4, elems_y, 4, levels).transpose(1, 3, 0, 2, 4, 5)
    nodes = nodes.reshape(element_count, fields, 16, levels)
    weights_in = to_cells.reshape(element_count, 4, 16)
    cells = jnp.einsum("epn,efnl->efpl", weights_in, nodes, preferred_element_type=jnp.float32)
    half_levels = levels // 2

    def own_levels(array):
        return lax.dynamic_slice_in_dim(array, member * half_levels, half_levels, array.ndim - 1)

    mixed = jnp.einsum("sfpl,lm->sfpm", cells, own_levels(vertical_map), precision=highest)
    response = jnp.einsum("gf,sfpl->sgpl", coupling, jnp.tanh(mixed), precision=highest)
    damping = own_levels(relaxation)[None, :, None, :] * (
        own_levels(cells)[:, :ntend] - mixed[:, :ntend]
    )
    element_tend = (response - damping + local_forcing[..., None]).astype(jnp.bfloat16)
    weights_out = to_nodes.reshape(element_count, 16, 4)
    nodal = jnp.einsum(
        "enp,egpl->egnl", weights_out, element_tend, preferred_element_type=jnp.float32
    )
    nodal = nodal.reshape(elems_x, elems_y, ntend, 4, 4, half_levels).transpose(2, 0, 3, 1, 4, 5)
    nodal = nodal.reshape(ntend, extent_x, extent_y, half_levels)
    advanced = own_levels(advanced)
    updated = advanced[:ntend].astype(jnp.float32) + dt_physics * nodal
    return jnp.concatenate([updated.astype(jnp.bfloat16), advanced[ntend:]], axis=0)


def solution(mesh):
    in_specs = (
        P("grp", None, "gx", "gy", None),
        P("gx", "gy", None, None),
        P("gx", "gy", None, None),
        P("gx", "gy", None, None),
        P("gx", "gy", None, None, None),
        P(),
        P(),
        P(),
    )
    out_specs = P(None, "gx", "gy", "grp")
    return jax.shard_map(shards, mesh=mesh, in_specs=in_specs, out_specs=out_specs, check_vma=False)
```

```python
import functools

import jax
import jax.numpy as jnp
import numpy as np
from jax import lax
from jax.experimental import pallas as pl
from jax.experimental.pallas import tpu as pltpu
from jax.sharding import PartitionSpec as P

f32 = jnp.float32
bf16 = jnp.bfloat16
MESH = pl.DeviceIdType.MESH
HBM = pl.BlockSpec(memory_space=pl.ANY)
VMEM = pl.BlockSpec(memory_space=pltpu.VMEM)
SMEM = pl.BlockSpec(memory_space=pltpu.SMEM)

NF, NTEND, LEV = 10, 8, 128
PAIRS = NF // 2
XROWS, YROWS = 16, 32
BLOCKS = XROWS // 4
NODES = 4 * YROWS
CELLS = YROWS
CX, CZ, CY = 4, 8, 4
DT_DYN, DT_PHY = 0.1, 0.25


def gll_matrix():
    points = np.array([-1.0, -1.0 / np.sqrt(5.0), 1.0 / np.sqrt(5.0), 1.0])
    bary = np.ones(4)
    for i in range(4):
        for j in range(4):
            if i != j:
                bary[i] /= points[i] - points[j]
    matrix = np.zeros((4, 4))
    for i in range(4):
        for j in range(4):
            if i != j:
                matrix[i, j] = bary[j] / bary[i] / (points[i] - points[j])
        matrix[i, i] = -np.sum(matrix[i])
    return matrix


def constants():
    d = gll_matrix()
    weight1 = np.array([0.5, 1.0, 1.0, 0.5])
    weight = np.kron(weight1, np.tile(weight1, YROWS // 4))
    along_x = np.kron(d, np.eye(YROWS))
    along_y = np.kron(np.eye(4 * YROWS // 4), d)
    both = np.concatenate([along_x, along_y]) * (-DT_DYN * np.tile(weight, 2))[:, None]
    high = np.asarray(both, np.float32).astype(jnp.bfloat16)
    low = (both - high.astype(np.float64)).astype(np.float32).astype(jnp.bfloat16)
    derive = np.concatenate([high, low], axis=1)
    share = np.eye(YROWS)
    for y in range(3, YROWS - 1, 4):
        share[y, y + 1] = share[y + 1, y] = 1.0
    advance = np.concatenate([np.kron(np.eye(4), share), np.eye(NODES)], axis=1)
    edges = np.zeros((BLOCKS, NODES, 2 * XROWS))
    for block in range(BLOCKS):
        for i in range(4):
            edges[block, i * YROWS, 4 * block + i] = 1.0
            edges[block, i * YROWS + YROWS - 1, XROWS + 4 * block + i] = 1.0
    return derive, advance.astype(jnp.bfloat16), edges.astype(jnp.bfloat16)


def iota(shape, dim):
    return lax.broadcasted_iota(jnp.int32, shape, dim)


def halves(x):
    high = x.astype(bf16)
    return high, (x - high.astype(f32)).astype(bf16)


def mm(a, b):
    return jnp.dot(a, b, preferred_element_type=f32)


def mm_nt(a, b):
    return lax.dot_general(a, b, (((1,), (1,)), ((), ())), preferred_element_type=f32)


def mm2(a, b):
    high, low = halves(b)
    return mm(a, high) + mm(a, low)


def main_kernel(
    sec, tc, tn, own, frc, vmap, cpl, rel, derive_h, advance_h, edges_h,
    packed, landed,
    both, adv, advd, wind, xlo, xhi, yrow, ysend, ylo, yhi, halo, csend, crecv,
    tc_v, tn_v, own_v, frc_v, v_v, rel_v, derive, advance, edges,
    f2, ts, win, wout, vv, fa, fb1, fs2, fb2, fs3, fb3, fbc, cells, split, mixed, act, tend,
    small_sem, local_sem, in_send, in_recv, e_send, e_recv, c_send, c_recv, f_send, f_recv,
    o_send, o_recv,
):
    m, gx, gy = lax.axis_index("grp"), lax.axis_index("gx"), lax.axis_index("gy")
    z, x = gx // CX, gx % CX
    ngx = CX * CZ
    other = 1 - m
    partner = (other, gx, gy)
    left_gx, right_gx = (gx + ngx - other) % ngx, (gx + m) % ngx
    cross_gx = (gx + ngx + 2 * m - 1) % ngx
    down, up = (gy + CY - 1) % CY, (gy + 1) % CY

    barrier = pltpu.get_barrier_semaphore()
    peers = [partner, (other, cross_gx, gy)]
    peers += [(other, a, b) for a in (gx, cross_gx) for b in (down, up)]
    peers += [(m, gx, (gy + j) % CY) for j in range(1, CY)]
    peers += [(m, z * CX + (x + j) % CX, gy) for j in range(1, CX)]
    peers += [(m, ((z + j) % CZ) * CX + x, gy) for j in range(1, CZ)]
    for peer in peers:
        pl.semaphore_signal(barrier, inc=1, device_id=peer, device_id_type=MESH)

    def local_in(p):
        return pltpu.make_async_copy(
            sec.at[0, pl.ds(2 * p, 2), pl.ds(m * XROWS, XROWS)],
            both.at[m, pl.ds(2 * p, 2)],
            local_sem.at[p],
        )

    def remote_in(p):
        return pltpu.make_async_remote_copy(
            sec.at[0, pl.ds(2 * p, 2), pl.ds(other * XROWS, XROWS)],
            both.at[m, pl.ds(2 * p, 2)],
            in_send.at[p], in_recv.at[p], device_id=partner, device_id_type=MESH,
        )

    def remote_in_wait(p):
        pltpu.make_async_remote_copy(
            both.at[other, pl.ds(2 * p, 2)],
            both.at[other, pl.ds(2 * p, 2)],
            in_send.at[p], in_recv.at[p], device_id=partner, device_id_type=MESH,
        ).wait_recv()

    small = [
        pltpu.make_async_copy(src, dst, small_sem.at[k])
        for k, (src, dst) in enumerate([
            (frc, frc_v), (derive_h, derive), (advance_h, advance), (edges_h, edges),
            (tc.at[pl.ds(m * BLOCKS, BLOCKS)], tc_v), (tn.at[pl.ds(m * BLOCKS, BLOCKS)], tn_v),
            (own, own_v), (vmap, v_v), (rel, rel_v),
        ])
    ]
    small[0].start()
    for p in range(PAIRS):
        local_in(p).start()
    for copy in small[1:]:
        copy.start()

    pl.semaphore_wait(barrier, len(peers))
    for p in range(PAIRS):
        remote_in(p).start()

    small[0].wait()
    for g in range(NTEND):
        f2[4 * g:4 * g + 4, :] = frc_v[g]
    source = iota((128, 256), 0)
    source = 2 * ((source % 32) * CY + source // 32)
    slot = iota((128, 256), 1)
    table = f2[...]
    rows_high, rows_low = halves(table)
    empty = jnp.zeros((32, 256), bf16)
    total = jnp.zeros((128, 128), f32)
    for r in range(2):
        pick = (slot == source + r).astype(f32).astype(bf16)
        for part in (rows_high, rows_low):
            stack = [empty] * 4
            stack[r] = part
            total = total + mm_nt(pick, jnp.concatenate(stack, axis=0))
    fa[...] = total

    def hops(k, src, dst, me, count, rows, device_of):
        out, arrive = [], []
        for j in range(1, count):
            to, frm = (me + j) % count, (me + count - j) % count
            for lst, dst_index in ((out, me), (arrive, frm)):
                lst.append(pltpu.make_async_remote_copy(
                    src.at[pl.ds(pl.multiple_of(to * rows, rows), rows)],
                    dst.at[pl.ds(pl.multiple_of(dst_index * rows, rows), rows)],
                    f_send.at[k, j], f_recv.at[k, j],
                    device_id=device_of(to), device_id_type=MESH,
                ))
        for copy in out:
            copy.start()
        mine = pl.ds(pl.multiple_of(me * rows, rows), rows)
        dst[mine, :] = src[mine, :]
        return out, arrive

    hop1, come1 = hops(0, fa, fb1, gy, CY, 32, lambda t: (m, gx, t))

    for copy in small[1:]:
        copy.wait()
    spread = (iota((16, 128), 0) == (iota((16, 128), 1) // 32) * 4 + iota((16, 128), 1) % 4)
    spread = spread.astype(f32).astype(bf16)
    inside = (iota((128, 128), 0) // 4) % 8 == (iota((128, 128), 1) // 4) % 8
    for k, ref in enumerate((tc_v, tn_v)):
        for block in range(BLOCKS):
            for ey in range(8):
                row = block * 32 + ey * 4
                ts[row:row + 4, :] = ref[block, ey].astype(f32)
        wide = jnp.where(inside, mm(ts[...].astype(bf16), spread), 0.0)
        if k == 0:
            win[...] = wide.astype(bf16)
        else:
            turned = jnp.transpose(wide * DT_PHY)
            eye = (iota((128, 128), 0) == iota((128, 128), 1)).astype(f32).astype(bf16)
            for block in range(BLOCKS):
                moved = turned if block == 0 else pltpu.roll(turned, 128 - 32 * block, 1)
                wout[block, :, 0:128] = eye
                wout[block, :, 128:256] = moved.astype(bf16)
    v_high, v_low = halves(v_v[...])
    vv[0:128, 0:128] = v_high
    vv[128:256, 0:128] = v_high
    vv[0:128, 128:256] = v_low
    vv[128:256, 128:256] = jnp.zeros((128, 128), bf16)

    for copy in come1:
        copy.wait_recv()
    for k in range(CX):
        fs2[32 * k:32 * k + 32, :] = fb1[pl.ds(k, 32, stride=CX), :]
    hop2, come2 = hops(1, fs2, fb2, x, CX, 32, lambda t: (m, z * CX + t, gy))

    def edge_copies(p):
        fields = pl.ds(2 * p, 2)
        return [
            pltpu.make_async_remote_copy(
                src, dst, e_send.at[k, p], e_recv.at[k, p], device_id=to, device_id_type=MESH
            )
            for k, (src, dst, to) in enumerate([
                (adv.at[fields, 0], xhi.at[fields], (other, left_gx, gy)),
                (adv.at[fields, XROWS - 1], xlo.at[fields], (other, right_gx, gy)),
                (ysend.at[0, fields], yhi.at[fields], (m, gx, down)),
                (ysend.at[1, fields], ylo.at[fields], (m, gx, up)),
            ])
        ]

    def section_pair(p, carry):
        @pl.when(m == 0)
        def _():
            local_in(p).wait()

        @pl.when(m == 1)
        def _():
            remote_in_wait(p)

        @pl.when(p == 0)
        def _():
            for k in range(2):
                for block in range(BLOCKS):
                    rows = both[0, k, 4 * block:4 * block + 4].reshape(NODES, LEV)
                    wind[k, block] = rows.astype(f32)

        def put(row, value, raw):
            for k in range(2):
                part = value[:, k * LEV:(k + 1) * LEV]
                f = 2 * p + k
                adv[f, row] = part.astype(bf16)
                for side, edge in ((0, 0), (1, YROWS - 1)):
                    line = part[edge:edge + 1, :]
                    yrow[side, k, row:row + 1, :] = line
                    if raw is not None:
                        csend[2 * raw + side, pl.ds(f, 1), :] = line

        last = None
        for block in range(BLOCKS):
            pair = [both[0, 2 * p + k, 4 * block:4 * block + 4].reshape(NODES, LEV) for k in range(2)]
            once = jnp.concatenate(pair, axis=1)
            slopes = mm(derive[...], jnp.concatenate([once, once], axis=0))
            u, v = wind[0, block], wind[1, block]
            value = jnp.concatenate([u, u], axis=1) * slopes[:NODES]
            value = value + jnp.concatenate([v, v], axis=1) * slopes[NODES:]
            first = value[:YROWS]
            if block == 0:
                put(0, first, 0)
            else:
                shared = last + first
                put(4 * block - 1, shared, None)
                put(4 * block, shared, None)
            put(4 * block + 1, value[YROWS:2 * YROWS], None)
            put(4 * block + 2, value[2 * YROWS:3 * YROWS], None)
            last = value[3 * YROWS:]
        put(XROWS - 1, last, 1)
        for side in range(2):
            for k in range(2):
                ysend[side, 2 * p + k] = yrow[side, k].astype(bf16)
        for copy in edge_copies(p):
            copy.start()
        return carry

    lax.fori_loop(0, PAIRS, section_pair, 0)

    corners = []
    for xs in range(2):
        for ys in range(2):
            corners.append(pltpu.make_async_remote_copy(
                csend.at[2 * xs + ys], crecv.at[3 - 2 * xs - ys],
                c_send.at[2 * xs + ys], c_recv.at[2 * xs + ys],
                device_id=(other, (left_gx, right_gx)[xs], (down, up)[ys]), device_id_type=MESH,
            ))
    for copy in corners:
        copy.start()

    for copy in come2:
        copy.wait_recv()
    for k in range(CZ):
        fs3[16 * k:16 * k + 16, :] = fb2[pl.ds(k, 16, stride=CZ), :]
    hop3, come3 = hops(2, fs3, fb3, z, CZ, 16, lambda t: (m, t * CX + x, gy))

    owned = (iota((128, 64), 0) == own_v[...]).astype(f32)
    before = (iota((64, 64), 0) < iota((64, 64), 1)).astype(f32).astype(bf16)
    rank = mm(owned.astype(bf16), before)
    mine = (iota((128, 64), 1) == m * 32 + iota((128, 64), 0) // 4).astype(f32).astype(bf16)
    from0 = mm_nt(mine, jnp.where(rank < 0.5, owned, 0.0).astype(bf16)).astype(bf16)
    from1 = mm_nt(mine, jnp.where(rank < 0.5, 0.0, owned).astype(bf16)).astype(bf16)

    for copy in come3:
        copy.wait_recv()
    table = fb3[...]
    lines = mm2(from0, table) + mm2(from1, pltpu.roll(table, 96, 1))
    lane = iota((128, 128), 1)
    lines = jnp.where((lane < 32) & (lane % 4 == iota((128, 128), 0) % 4), lines, 0.0)
    high = lines.astype(bf16).astype(f32)
    lines = (high + pltpu.roll(lines - high, 32, 1)).astype(bf16)
    group = jnp.where(iota((128, 128), 0) < 64, (iota((128, 128), 0) // 4) % 8, 8)
    for g in range(NTEND):
        fbc[g] = mm(lines, (group == g).astype(f32).astype(bf16))

    for copy in corners:
        copy.wait_recv()

    def halo_pair(p, carry):
        for copy in edge_copies(p):
            copy.wait_recv()

        @pl.when(m == 1)
        def _():
            local_in(p).wait()

        @pl.when(m == 0)
        def _():
            remote_in_wait(p)

        at = iota((XROWS, LEV), 0)
        for k in range(2):
            f = 2 * p + k
            for side, ref in ((0, ylo), (1, yhi)):
                first = jnp.broadcast_to(crecv[side, pl.ds(f, 1), :], (XROWS, LEV))
                final = jnp.broadcast_to(crecv[2 + side, pl.ds(f, 1), :], (XROWS, LEV))
                value = ref[f].astype(f32)
                value = value + jnp.where(at == 0, first, jnp.where(at == XROWS - 1, final, 0.0))
                halo[f, side * XROWS:(side + 1) * XROWS, :] = value.astype(bf16)
        return carry

    lax.fori_loop(0, PAIRS, halo_pair, 0)

    lower = iota((YROWS, LEV), 1) < LEV // 2

    def pack(block, f, value):
        for i in range(2):
            a = value[i * YROWS:(i + 1) * YROWS]
            b = value[(i + 2) * YROWS:(i + 3) * YROWS]
            packed[0, block, f, i] = jnp.where(lower, a, pltpu.roll(b, 64, 1)).astype(bf16)
            packed[1, block, f, i] = jnp.where(lower, pltpu.roll(a, 64, 1), b).astype(bf16)

    def out_copy(block):
        return pltpu.make_async_remote_copy(
            packed.at[other, block], landed.at[block], o_send.at[block], o_recv.at[block],
            device_id=partner, device_id_type=MESH,
        )

    for block in (1, 2, 0, 3):
        weights = win[32 * block:32 * block + 32, :]

        def advance_pair(p, carry):
            parts, starts = [], []
            for k in range(2):
                f = 2 * p + k
                rows = [adv[f, 4 * block + i] for i in range(4)]
                if block == 0:
                    rows[0] = (rows[0].astype(f32) + xlo[f].astype(f32)).astype(bf16)
                if block == BLOCKS - 1:
                    rows[3] = (rows[3].astype(f32) + xhi[f].astype(f32)).astype(bf16)
                start = both[1, f, 4 * block:4 * block + 4].reshape(NODES, LEV)
                parts.append(jnp.concatenate(rows + [start], axis=0))
                starts.append(halo[f])
            value = mm(advance[...], jnp.concatenate(parts, axis=1))
            value = value + mm(edges[block], jnp.concatenate(starts, axis=1))
            value = value.astype(bf16)
            got = mm(weights, value)
            for k in range(2):
                f = 2 * p + k
                advd[f, block] = value[:, k * LEV:(k + 1) * LEV]
                one = got[:, k * LEV:(k + 1) * LEV]
                cells[f] = one
                high, low = halves(one)
                split[f, :, 0:LEV] = high
                split[f, :, LEV:2 * LEV] = low
            return carry

        lax.fori_loop(0, PAIRS, advance_pair, 0)

        def mix_pair(p, carry):
            lhs = split[pl.ds(2 * p, 2)].reshape(2 * CELLS, 2 * LEV)
            got = mm(lhs, vv[...])
            got = got[:, :LEV] + got[:, LEV:]
            warm = jnp.tanh(got)
            for k in range(2):
                mixed[2 * p + k] = got[k * CELLS:(k + 1) * CELLS]
                act[2 * p + k] = warm[k * CELLS:(k + 1) * CELLS]
            return carry

        lax.fori_loop(0, PAIRS, mix_pair, 0, unroll=True)

        for g in range(NTEND):
            acc = fbc[g, 32 * block:32 * block + 32, :]
            for f in range(NF):
                acc = acc + cpl[g, f] * act[f]
            acc = acc - rel_v[g:g + 1, :] * (cells[g] - mixed[g])
            tend[g] = acc.astype(bf16)

        def update_pair(p, carry):
            parts = [
                jnp.concatenate([advd[2 * p + k, block], tend[2 * p + k]], axis=0) for k in range(2)
            ]
            value = mm(wout[block, :, 0:NODES + CELLS], jnp.concatenate(parts, axis=1))
            for k in range(2):
                pack(block, 2 * p + k, value[:, k * LEV:(k + 1) * LEV])
            return carry

        lax.fori_loop(0, NTEND // 2, update_pair, 0)
        for f in range(NTEND, NF):
            pack(block, f, advd[f, block].astype(f32))
        out_copy(block).start()

    for p in range(PAIRS):
        remote_in(p).wait_send()
        for copy in edge_copies(p):
            copy.wait_send()
    for copy in corners + hop1 + hop2 + hop3:
        copy.wait_send()
    for block in range(BLOCKS):
        out_copy(block).wait_send()
        out_copy(block).wait_recv()


def main_call(args):
    v = pltpu.VMEM
    packed_shape = (BLOCKS, NF, 2, YROWS, LEV)
    dma = pltpu.SemaphoreType.DMA
    scratch = [
        v((2, NF, XROWS, YROWS, LEV), bf16),
        v((NF, XROWS, YROWS, LEV), bf16),
        v((NF, BLOCKS, NODES, LEV), bf16),
        v((2, BLOCKS, NODES, LEV), f32),
        v((NF, YROWS, LEV), bf16),
        v((NF, YROWS, LEV), bf16),
        v((2, 2, XROWS, LEV), f32),
        v((2, NF, XROWS, LEV), bf16),
        v((NF, XROWS, LEV), bf16),
        v((NF, XROWS, LEV), bf16),
        v((NF, 2 * XROWS, LEV), bf16),
        v((4, 16, LEV), f32),
        v((4, 16, LEV), f32),
        v((BLOCKS, 8, 4, 16), bf16),
        v((BLOCKS, 8, 4, 16), bf16),
        v((1, 64), jnp.int32),
        v((NTEND, 4, 256), f32),
        v((LEV, LEV), f32),
        v((NTEND, LEV), f32),
        v((2 * NODES, 2 * NODES), bf16),
        v((NODES, 2 * NODES), bf16),
        v((BLOCKS, NODES, 2 * XROWS), bf16),
        v((32, 256), f32),
        v((128, 16), f32),
        v((128, 128), bf16),
        v((BLOCKS, 128, 256), bf16),
        v((256, 256), bf16),
    ]
    scratch += [v((128, 128), f32)] * 6
    scratch += [
        v((NTEND, 128, LEV), f32),
        v((NF, CELLS, LEV), f32),
        v((NF, CELLS, 2 * LEV), bf16),
        v((NF, CELLS, LEV), f32),
        v((NF, CELLS, LEV), f32),
        v((NTEND, CELLS, LEV), bf16),
        dma((9,)), dma((PAIRS,)), dma((PAIRS,)), dma((PAIRS,)),
        dma((4, PAIRS)), dma((4, PAIRS)), dma((4,)), dma((4,)),
        dma((3, CZ)), dma((3, CZ)), dma((BLOCKS,)), dma((BLOCKS,)),
    ]
    in_specs = [HBM] * 11
    in_specs[6] = SMEM
    return pl.pallas_call(
        main_kernel,
        out_shape=(
            jax.ShapeDtypeStruct((2,) + packed_shape, bf16),
            jax.ShapeDtypeStruct(packed_shape, bf16),
        ),
        in_specs=in_specs,
        out_specs=(VMEM, VMEM),
        scratch_shapes=scratch,
        compiler_params=pltpu.CompilerParams(
            collective_id=0, has_side_effects=True, vmem_limit_bytes=40 * 2**20
        ),
    )(*args)


def unpack_kernel(packed, landed, out, stage, sems):
    m = lax.axis_index("grp")

    def copy(k, block):
        rows = (m if k == 0 else 1 - m) * XROWS + 4 * block
        return pltpu.make_async_copy(
            stage.at[k, block], out.at[:, pl.ds(rows, 4)], sems.at[k, block]
        )

    for k in range(2):
        for block in range(BLOCKS):

            def one(f, carry):
                for i in range(2):
                    line = packed[m, block, f, i] if k == 0 else landed[block, f, i]
                    stage[k, block, f, i] = line[:, :LEV // 2]
                    moved = pltpu.roll(line.astype(f32), 64, 1).astype(bf16)
                    stage[k, block, f, i + 2] = moved[:, :LEV // 2]
                return carry

            lax.fori_loop(0, NF, one, 0, unroll=True)
            copy(k, block).start()
    for k in range(2):
        for block in range(BLOCKS):
            copy(k, block).wait()


def unpack_call(packed, landed):
    return pl.pallas_call(
        unpack_kernel,
        out_shape=jax.ShapeDtypeStruct((NF, 2 * XROWS, YROWS, LEV // 2), bf16),
        in_specs=[VMEM, VMEM],
        out_specs=HBM,
        scratch_shapes=[
            pltpu.VMEM((2, BLOCKS, NF, 4, YROWS, LEV // 2), bf16),
            pltpu.SemaphoreType.DMA((2, BLOCKS)),
        ],
        compiler_params=pltpu.CompilerParams(vmem_limit_bytes=24 * 2**20),
    )(packed, landed)


def shards(
    section_levels, to_cells, to_nodes, owner_map, forcing, vertical_map, coupling, relaxation
):
    derive, advance, edges = (jnp.asarray(c) for c in constants())
    packed, landed = main_call((
        section_levels, to_cells, jnp.swapaxes(to_nodes, 2, 3), owner_map.reshape(1, 64),
        forcing[0, 0], vertical_map, coupling, relaxation, derive, advance, edges,
    ))
    return unpack_call(packed, landed)


def solution(mesh):
    in_specs = (
        P("grp", None, "gx", "gy", None),
        P("gx", "gy", None, None),
        P("gx", "gy", None, None),
        P("gx", "gy", None, None),
        P("gx", "gy", None, None, None),
        P(),
        P(),
        P(),
    )
    out_specs = P(None, "gx", "gy", "grp")
    return jax.shard_map(shards, mesh=mesh, in_specs=in_specs, out_specs=out_specs, check_vma=False)
```

```python
import functools

import jax
import jax.numpy as jnp
import numpy as np
from jax import lax
from jax.experimental import pallas as pl
from jax.experimental.pallas import tpu as pltpu
from jax.sharding import PartitionSpec as P

f32 = jnp.float32
bf16 = jnp.bfloat16
MESH = pl.DeviceIdType.MESH
HBM = pl.BlockSpec(memory_space=pltpu.HBM)
VMEM = pl.BlockSpec(memory_space=pltpu.VMEM)
SMEM = pl.BlockSpec(memory_space=pltpu.SMEM)

NF, NTEND, LEV = 10, 8, 128
PAIRS = NF // 2
XROWS, YROWS = 16, 32
BLOCKS = XROWS // 4
NODES = 4 * YROWS
CELLS = YROWS
CX, CZ, CY = 4, 8, 4
DT_DYN, DT_PHY = 0.1, 0.25


def gll_matrix():
    points = np.array([-1.0, -1.0 / np.sqrt(5.0), 1.0 / np.sqrt(5.0), 1.0])
    bary = np.ones(4)
    for i in range(4):
        for j in range(4):
            if i != j:
                bary[i] /= points[i] - points[j]
    matrix = np.zeros((4, 4))
    for i in range(4):
        for j in range(4):
            if i != j:
                matrix[i, j] = bary[j] / bary[i] / (points[i] - points[j])
        matrix[i, i] = -np.sum(matrix[i])
    return matrix


def constants():
    d = gll_matrix()
    weight1 = np.array([0.5, 1.0, 1.0, 0.5])
    weight = np.kron(weight1, np.tile(weight1, YROWS // 4))
    along_x = np.kron(d, np.eye(YROWS))
    along_y = np.kron(np.eye(4 * YROWS // 4), d)
    both = np.concatenate([along_x, along_y]) * (-DT_DYN * np.tile(weight, 2))[:, None]
    high = np.asarray(both, np.float32).astype(jnp.bfloat16)
    low = (both - high.astype(np.float64)).astype(np.float32).astype(jnp.bfloat16)
    derive = np.concatenate([high, low], axis=1)
    share = np.eye(YROWS)
    for y in range(3, YROWS - 1, 4):
        share[y, y + 1] = share[y + 1, y] = 1.0
    advance = np.concatenate([np.kron(np.eye(4), share), np.eye(NODES)], axis=1)
    edges = np.zeros((BLOCKS, NODES, 2 * XROWS))
    for block in range(BLOCKS):
        for i in range(4):
            edges[block, i * YROWS, 4 * block + i] = 1.0
            edges[block, i * YROWS + YROWS - 1, XROWS + 4 * block + i] = 1.0
    return derive, advance.astype(jnp.bfloat16), edges.astype(jnp.bfloat16)


def iota(shape, dim):
    return lax.broadcasted_iota(jnp.int32, shape, dim)


def halves(x):
    high = x.astype(bf16)
    return high, (x - high.astype(f32)).astype(bf16)


def mm(a, b):
    return jnp.dot(a, b, preferred_element_type=f32)


def mm_nt(a, b):
    return lax.dot_general(a, b, (((1,), (1,)), ((), ())), preferred_element_type=f32)


def mm2(a, b):
    high, low = halves(b)
    return mm(a, high) + mm(a, low)


def main_kernel(
    sec, tc, tn, own, frc, vmap, cpl, rel, derive_h, advance_h, edges_h,
    packed, landed,
    cur, start, adv, advx, advd, wind, xlo, xhi, yrow, ysend, ylo, yhi, halo, csend, clo, chi,
    tc_v, tn_v, own_v, frc_v, v_v, rel_v, cpl_v, derive, advance, edges,
    f2, ts, win, wout, vv, fa, fb1, fs2, fb2, fbc, cells, split, mixed, act, base, tend,
    small_sem, q_sem, s_send, s_recv, e_send, e_recv, c_send, c_recv, f_send, f_recv,
    o_send, o_recv,
):
    m, gx, gy = lax.axis_index("grp"), lax.axis_index("gx"), lax.axis_index("gy")
    z, x = gx // CX, gx % CX
    ngx = CX * CZ
    other = 1 - m
    partner = (other, gx, gy)
    left, right = (gx + ngx - 1) % ngx, (gx + 1) % ngx
    down, up = (gy + CY - 1) % CY, (gy + 1) % CY

    def plane_peer(j):
        return (1, z * CX + (x + j // CY) % CX, (gy + j % CY) % CY)

    def line_peer(member, j):
        return (member, ((z + j) % CZ) * CX + x, gy)

    barrier = pltpu.get_barrier_semaphore()

    def greet(peers):
        for peer in peers:
            pl.semaphore_signal(barrier, inc=1, device_id=peer, device_id_type=MESH)

    @pl.when(m == 0)
    def _():
        greet([partner, (0, left, gy), (0, gx, down), (0, gx, up), (0, left, down), (0, left, up)])
        greet([line_peer(1, j) for j in range(1, CZ)])

    @pl.when(m == 1)
    def _():
        greet([partner, (0, right, gy), (0, gx, down), (0, gx, up), (0, right, down), (0, right, up)])
        greet([plane_peer(j) for j in range(1, CX * CY)])
        greet([line_peer(1, j) for j in range(1, CZ)])

    small = [
        pltpu.make_async_copy(src, dst, small_sem.at[k])
        for k, (src, dst) in enumerate([
            (frc, frc_v), (derive_h, derive), (advance_h, advance), (edges_h, edges),
            (tc.at[pl.ds(m * BLOCKS, BLOCKS)], tc_v), (tn.at[pl.ds(m * BLOCKS, BLOCKS)], tn_v),
            (own, own_v), (vmap, v_v), (rel, rel_v), (cpl, cpl_v),
        ])
    ]

    def current_in(p):
        fields = pl.ds(2 * p, 2)
        return pltpu.make_async_copy(sec.at[0, fields], cur.at[fields], q_sem.at[p])

    def start_in(p):
        fields = pl.ds(2 * p, 2)
        return pltpu.make_async_copy(
            sec.at[0, fields, pl.ds(XROWS, XROWS)], start.at[fields], s_recv.at[p]
        )

    def start_out(p):
        fields = pl.ds(2 * p, 2)
        return pltpu.make_async_remote_copy(
            sec.at[0, fields, pl.ds(0, XROWS)], start.at[fields], s_send.at[p], s_recv.at[p],
            device_id=partner, device_id_type=MESH,
        )

    def start_wait(p):
        fields = start.at[pl.ds(2 * p, 2)]
        pltpu.make_async_copy(fields, fields, s_recv.at[p]).wait()

    def edge_copies(p, kinds=range(7)):
        fields = pl.ds(2 * p, 2)
        return [
            pltpu.make_async_remote_copy(
                src, dst, e_send.at[k, p], e_recv.at[k, p], device_id=to, device_id_type=MESH
            )
            for k, (src, dst, to) in enumerate([
                (advx.at[fields], adv.at[fields], (1, gx, gy)),
                (adv.at[fields, 0], xhi.at[fields], (1, left, gy)),
                (advx.at[fields, XROWS - 1], xlo.at[fields], (0, right, gy)),
                (ysend.at[0, 0, fields], yhi.at[fields], (0, gx, down)),
                (ysend.at[0, 1, fields], yhi.at[fields], (1, gx, down)),
                (ysend.at[1, 0, fields], ylo.at[fields], (0, gx, up)),
                (ysend.at[1, 1, fields], ylo.at[fields], (1, gx, up)),
            ])
            if k in kinds
        ]

    def corner_copies(sides=(0, 1)):
        return [
            pltpu.make_async_remote_copy(
                csend.at[2 * xs + ys], (chi, clo)[xs].at[1 - ys], c_send.at[2 * xs + ys],
                c_recv.at[2 * xs + ys],
                device_id=(1 - xs, (left, right)[xs], (down, up)[ys]), device_id_type=MESH,
            )
            for xs in sides for ys in range(2)
        ]

    def plane_copy(j, arriving):
        _, tx, ty = plane_peer(j)
        to = (tx % CX) * CY + ty
        me = x * CY + gy
        if arriving:
            me = ((x + CX - j // CY) % CX) * CY + (gy + CY - j % CY) % CY
        return pltpu.make_async_remote_copy(
            fa.at[pl.ds(pl.multiple_of(to * 8, 8), 8)],
            fb1.at[pl.ds(pl.multiple_of(me * 8, 8), 8)],
            f_send.at[0, j], f_recv.at[0, j], device_id=plane_peer(j), device_id_type=MESH,
        )

    def line_copy(member, j, arriving=False):
        to, me = (z + j) % CZ, z
        if arriving:
            me = (z + CZ - j) % CZ
        return pltpu.make_async_remote_copy(
            fs2.at[pl.ds(pl.multiple_of(to * 16, 16), 16)],
            fb2.at[pl.ds(pl.multiple_of(me * 16, 16), 16)],
            f_send.at[1 + member, j], f_recv.at[1, j],
            device_id=line_peer(member, j), device_id_type=MESH,
        )

    @pl.when(m == 0)
    def _():
        for p in range(PAIRS):
            current_in(p).start()
        for copy in small:
            copy.start()
        small[1].wait()

        def put(p, row, value, raw):
            for k in range(2):
                part = value[:, k * LEV:(k + 1) * LEV]
                f = 2 * p + k
                if row < XROWS:
                    adv[f, row] = part.astype(bf16)
                else:
                    advx[f, row - XROWS] = part.astype(bf16)
                for side, edge in ((0, 0), (1, YROWS - 1)):
                    line = part[edge:edge + 1, :]
                    yrow[side, f, row:row + 1, :] = line
                    if raw is not None:
                        csend[2 * raw + side, f:f + 1, :] = line

        for p in range(PAIRS):
            current_in(p).wait()
            if p == 0:
                for k in range(2):
                    for block in range(2 * BLOCKS):
                        rows = cur[k, 4 * block:4 * block + 4].reshape(NODES, LEV)
                        wind[k, block] = rows.astype(f32)
            last = None
            for block in range(2 * BLOCKS):
                pair = [
                    cur[2 * p + k, 4 * block:4 * block + 4].reshape(NODES, LEV) for k in range(2)
                ]
                once = jnp.concatenate(pair, axis=1)
                slopes = mm(derive[...], jnp.concatenate([once, once], axis=0))
                u, v = wind[0, block], wind[1, block]
                value = jnp.concatenate([u, u], axis=1) * slopes[:NODES]
                value = value + jnp.concatenate([v, v], axis=1) * slopes[NODES:]
                first = value[:YROWS]
                if block == 0:
                    put(p, 0, first, 0)
                else:
                    shared = last + first
                    put(p, 4 * block - 1, shared, None)
                    put(p, 4 * block, shared, None)
                put(p, 4 * block + 1, value[YROWS:2 * YROWS], None)
                put(p, 4 * block + 2, value[2 * YROWS:3 * YROWS], None)
                last = value[3 * YROWS:]
            put(p, 2 * XROWS - 1, last, 1)
            for side in range(2):
                for k in range(2):
                    f = 2 * p + k
                    for half in range(2):
                        lines = yrow[side, f, half * XROWS:(half + 1) * XROWS]
                        ysend[side, half, f] = lines.astype(bf16)
            if p == SENT:
                pl.semaphore_wait(barrier, 11)
                for q in range(p):
                    for copy in edge_copies(q):
                        copy.start()
            if p >= SENT:
                for copy in edge_copies(p):
                    copy.start()
        for copy in corner_copies():
            copy.start()
        xhi[...] = jnp.zeros_like(xhi)
        chi[...] = jnp.zeros_like(chi)

    @pl.when(m == 1)
    def _():
        for p in range(PAIRS):
            start_in(p).start()
        for copy in small:
            copy.start()
        small[0].wait()
        for g in range(NTEND):
            f2[4 * g:4 * g + 4, :] = frc_v[g]
        source = iota((128, 256), 0)
        source = 2 * ((source % CZ) * (CX * CY) + source // CZ)
        slot = iota((128, 256), 1)
        rows_high, rows_low = halves(f2[...])
        empty = jnp.zeros((32, 256), bf16)
        total = jnp.zeros((128, 128), f32)
        for r in range(2):
            pick = (slot == source + r).astype(f32).astype(bf16)
            for part in (rows_high, rows_low):
                stack = [empty] * 4
                stack[r] = part
                total = total + mm_nt(pick, jnp.concatenate(stack, axis=0))
        fa[...] = total
        xlo[...] = jnp.zeros_like(xlo)
        clo[...] = jnp.zeros_like(clo)
        pl.semaphore_wait(barrier, 30)
        for j in range(1, CX * CY):
            plane_copy(j, False).start()
        for p in range(PAIRS):
            start_out(p).start()
        mine = pl.ds(pl.multiple_of((x * CY + gy) * 8, 8), 8)
        fb1[mine, :] = fa[mine, :]

    for copy in small[4:]:
        copy.wait()
    spread = (iota((16, 128), 0) == (iota((16, 128), 1) // 32) * 4 + iota((16, 128), 1) % 4)
    spread = spread.astype(f32).astype(bf16)
    inside = (iota((128, 128), 0) // 4) % 8 == (iota((128, 128), 1) // 4) % 8
    for k, ref in enumerate((tc_v, tn_v)):
        for block in range(BLOCKS):
            for ey in range(8):
                row = block * 32 + ey * 4
                ts[row:row + 4, :] = ref[block, ey].astype(f32)
        wide = jnp.where(inside, mm(ts[...].astype(bf16), spread), 0.0)
        if k == 0:
            win[...] = wide.astype(bf16)
        else:
            turned = jnp.transpose(wide * DT_PHY)
            eye = (iota((128, 128), 0) == iota((128, 128), 1)).astype(f32).astype(bf16)
            for block in range(BLOCKS):
                moved = turned if block == 0 else pltpu.roll(turned, 128 - 32 * block, 1)
                wout[block, :, 0:128] = eye
                wout[block, :, 128:256] = moved.astype(bf16)
    v_high, v_low = halves(v_v[...])
    vv[0:128, 0:128] = v_high
    vv[128:256, 0:128] = v_high
    vv[0:128, 128:256] = v_low
    vv[128:256, 128:256] = jnp.zeros((128, 128), bf16)

    owned = (iota((128, 64), 0) == own_v[...]).astype(f32)
    before = (iota((64, 64), 0) < iota((64, 64), 1)).astype(f32).astype(bf16)
    rank = mm(owned.astype(bf16), before)
    mine = (iota((128, 64), 1) == m * 32 + iota((128, 64), 0) // 4).astype(f32).astype(bf16)
    from0 = mm_nt(mine, jnp.where(rank < 0.5, owned, 0.0).astype(bf16)).astype(bf16)
    from1 = mm_nt(mine, jnp.where(rank < 0.5, 0.0, owned).astype(bf16)).astype(bf16)

    @pl.when(m == 0)
    def _():
        small[2].wait()
        small[3].wait()
        small[0].wait()
        for p in range(PAIRS):
            for copy in edge_copies(p, (2, 3, 5)):
                copy.wait_recv()
        for copy in corner_copies((1,)):
            copy.wait_recv()

    @pl.when(m == 1)
    def _():
        small[1].wait()
        small[2].wait()
        small[3].wait()
        for j in range(1, CX * CY):
            plane_copy(j, True).wait_recv()
        for k in range(CZ):
            fs2[16 * k:16 * k + 16, :] = fb1[pl.ds(k, 16, stride=CZ), :]
        for j in range(1, CZ):
            for member in range(2):
                line_copy(member, j).start()
        mine = pl.ds(pl.multiple_of(z * 16, 16), 16)
        pltpu.make_async_remote_copy(
            fs2.at[mine], fb2.at[mine], f_send.at[1, 0], f_recv.at[1, 0],
            device_id=partner, device_id_type=MESH,
        ).start()
        fb2[mine, :] = fs2[mine, :]
        for p in range(PAIRS):
            for copy in edge_copies(p, (0, 1, 4, 6)):
                copy.wait_recv()
        for copy in corner_copies((0,)):
            copy.wait_recv()

    for p in range(PAIRS):
        start_wait(p)
    at = iota((XROWS, LEV), 0)
    for f in range(NF):
        for side, ref in ((0, ylo), (1, yhi)):
            first = jnp.broadcast_to(clo[side, f:f + 1, :], (XROWS, LEV))
            final = jnp.broadcast_to(chi[side, f:f + 1, :], (XROWS, LEV))
            value = ref[f].astype(f32)
            value = value + jnp.where(at == 0, first, jnp.where(at == XROWS - 1, final, 0.0))
            halo[f, side * XROWS:(side + 1) * XROWS, :] = value.astype(bf16)

    for block in range(BLOCKS):
        weights = win[32 * block:32 * block + 32, :]
        for p in range(PAIRS):
            parts, starts = [], []
            for k in range(2):
                f = 2 * p + k
                rows = [adv[f, 4 * block + i] for i in range(4)]
                if block == 0:
                    rows[0] = (rows[0].astype(f32) + xlo[f].astype(f32)).astype(bf16)
                if block == BLOCKS - 1:
                    rows[3] = (rows[3].astype(f32) + xhi[f].astype(f32)).astype(bf16)
                begun = start[f, 4 * block:4 * block + 4].reshape(NODES, LEV)
                parts.append(jnp.concatenate(rows + [begun], axis=0))
                starts.append(halo[f])
            value = mm(advance[...], jnp.concatenate(parts, axis=1))
            value = value + mm(edges[block], jnp.concatenate(starts, axis=1))
            value = value.astype(bf16)
            got = mm(weights, value)
            for k in range(2):
                f = 2 * p + k
                advd[f, block] = value[:, k * LEV:(k + 1) * LEV]
                one = got[:, k * LEV:(k + 1) * LEV]
                cells[block, f] = one
                high, low = halves(one)
                split[block, f, :, 0:LEV] = high
                split[block, f, :, LEV:2 * LEV] = low
        for p in range(PAIRS):
            lhs = split[block, 2 * p:2 * p + 2].reshape(2 * CELLS, 2 * LEV)
            got = mm(lhs, vv[...])
            got = got[:, :LEV] + got[:, LEV:]
            warm = jnp.tanh(got)
            for k in range(2):
                mixed[block, 2 * p + k] = got[k * CELLS:(k + 1) * CELLS]
                act[block, 2 * p + k] = warm[k * CELLS:(k + 1) * CELLS]
        for g in range(NTEND):
            acc = rel_v[g:g + 1, :] * (mixed[block, g] - cells[block, g])
            for f in range(NF):
                acc = acc + cpl_v[g, f] * act[block, f]
            base[block, g] = acc

    @pl.when(m == 0)
    def _():
        for j in range(CZ):
            line_copy(0, j, True).wait_recv()

    @pl.when(m == 1)
    def _():
        for j in range(1, CZ):
            line_copy(1, j, True).wait_recv()

    table = fb2[...]
    lines = mm2(from0, table) + mm2(from1, pltpu.roll(table, 96, 1))
    lane = iota((128, 128), 1)
    lines = jnp.where((lane < 32) & (lane % 4 == iota((128, 128), 0) % 4), lines, 0.0)
    high = lines.astype(bf16).astype(f32)
    lines = (high + pltpu.roll(lines - high, 32, 1)).astype(bf16)
    group = jnp.where(iota((128, 128), 0) < 64, (iota((128, 128), 0) // 4) % 8, 8)
    for g in range(NTEND):
        fbc[g] = mm(lines, (group == g).astype(f32).astype(bf16))

    lower = iota((YROWS, LEV), 1) < LEV // 2

    def pack(block, f, value):
        for i in range(2):
            a = value[i * YROWS:(i + 1) * YROWS]
            b = value[(i + 2) * YROWS:(i + 3) * YROWS]
            packed[0, block, f, i] = jnp.where(lower, a, pltpu.roll(b, 64, 1)).astype(bf16)
            packed[1, block, f, i] = jnp.where(lower, pltpu.roll(a, 64, 1), b).astype(bf16)

    def out_copy(block):
        return pltpu.make_async_remote_copy(
            packed.at[other, block], landed.at[block], o_send.at[block], o_recv.at[block],
            device_id=partner, device_id_type=MESH,
        )

    for block in range(BLOCKS):
        for f in range(NTEND, NF):
            pack(block, f, advd[f, block].astype(f32))
        for g in range(NTEND):
            tend[block, g] = (base[block, g] + fbc[g, 32 * block:32 * block + 32, :]).astype(bf16)
        for p in range(NTEND // 2):
            parts = [
                jnp.concatenate([advd[2 * p + k, block], tend[block, 2 * p + k]], axis=0)
                for k in range(2)
            ]
            value = mm(wout[block, :, 0:NODES + CELLS], jnp.concatenate(parts, axis=1))
            for k in range(2):
                pack(block, 2 * p + k, value[:, k * LEV:(k + 1) * LEV])
        out_copy(block).start()

    @pl.when(m == 0)
    def _():
        for p in range(PAIRS):
            for copy in edge_copies(p):
                copy.wait_send()
        for copy in corner_copies():
            copy.wait_send()

    @pl.when(m == 1)
    def _():
        for p in range(PAIRS):
            start_out(p).wait_send()
        for j in range(1, CX * CY):
            plane_copy(j, False).wait_send()
        for j in range(1, CZ):
            for member in range(2):
                line_copy(member, j).wait_send()
        line_copy(0, 0).wait_send()

    for block in range(BLOCKS):
        out_copy(block).wait_send()
        out_copy(block).wait_recv()


SENT = 1


def main_call(args):
    v = pltpu.VMEM
    packed_shape = (BLOCKS, NF, 2, YROWS, LEV)
    dma = pltpu.SemaphoreType.DMA
    scratch = [
        v((NF, 2 * XROWS, YROWS, LEV), bf16),
        v((NF, XROWS, YROWS, LEV), bf16),
        v((NF, XROWS, YROWS, LEV), bf16),
        v((NF, XROWS, YROWS, LEV), bf16),
        v((NF, BLOCKS, NODES, LEV), bf16),
        v((2, 2 * BLOCKS, NODES, LEV), f32),
        v((NF, YROWS, LEV), bf16),
        v((NF, YROWS, LEV), bf16),
        v((2, NF, 2 * XROWS, LEV), f32),
        v((2, 2, NF, XROWS, LEV), bf16),
        v((NF, XROWS, LEV), bf16),
        v((NF, XROWS, LEV), bf16),
        v((NF, 2 * XROWS, LEV), bf16),
        v((4, 16, LEV), f32),
        v((2, 16, LEV), f32),
        v((2, 16, LEV), f32),
        v((BLOCKS, 8, 4, 16), bf16),
        v((BLOCKS, 8, 4, 16), bf16),
        v((1, 64), jnp.int32),
        v((NTEND, 4, 256), f32),
        v((LEV, LEV), f32),
        v((NTEND, LEV), f32),
        pltpu.SMEM((NTEND, NF), f32),
        v((2 * NODES, 2 * NODES), bf16),
        v((NODES, 2 * NODES), bf16),
        v((BLOCKS, NODES, 2 * XROWS), bf16),
        v((32, 256), f32),
        v((128, 16), f32),
        v((128, 128), bf16),
        v((BLOCKS, 128, 256), bf16),
        v((256, 256), bf16),
    ]
    scratch += [v((128, 128), f32)] * 4
    scratch += [
        v((NTEND, 128, LEV), f32),
        v((BLOCKS, NF, CELLS, LEV), f32),
        v((BLOCKS, NF, CELLS, 2 * LEV), bf16),
        v((BLOCKS, NF, CELLS, LEV), f32),
        v((BLOCKS, NF, CELLS, LEV), f32),
        v((BLOCKS, NTEND, CELLS, LEV), f32),
        v((BLOCKS, NTEND, CELLS, LEV), bf16),
        dma((10,)), dma((PAIRS,)), dma((PAIRS,)), dma((PAIRS,)),
        dma((7, PAIRS)), dma((7, PAIRS)), dma((4,)), dma((4,)),
        dma((3, CX * CY)), dma((2, CX * CY)), dma((BLOCKS,)), dma((BLOCKS,)),
    ]
    return pl.pallas_call(
        main_kernel,
        out_shape=(
            jax.ShapeDtypeStruct((2,) + packed_shape, bf16),
            jax.ShapeDtypeStruct(packed_shape, bf16),
        ),
        in_specs=[HBM] * 11,
        out_specs=(VMEM, VMEM),
        scratch_shapes=scratch,
        compiler_params=pltpu.CompilerParams(
            collective_id=0, has_side_effects=True, vmem_limit_bytes=40 * 2**20
        ),
    )(*args)


def unpack_kernel(packed, landed, out, stage, sems):
    m = lax.axis_index("grp")

    def copy(k, block):
        rows = (m if k == 0 else 1 - m) * XROWS + 4 * block
        return pltpu.make_async_copy(
            stage.at[k, block], out.at[:, pl.ds(rows, 4)], sems.at[k, block]
        )

    for k in range(2):
        for block in range(BLOCKS):

            def one(f):
                for i in range(2):
                    line = packed[m, block, f, i] if k == 0 else landed[block, f, i]
                    stage[k, block, f, i] = line[:, :LEV // 2]
                    moved = pltpu.roll(line.astype(f32), 64, 1).astype(bf16)
                    stage[k, block, f, i + 2] = moved[:, :LEV // 2]

            for step in range(NF):
                one(step)
            copy(k, block).start()
    for k in range(2):
        for block in range(BLOCKS):
            copy(k, block).wait()


def unpack_call(packed, landed):
    return pl.pallas_call(
        unpack_kernel,
        out_shape=jax.ShapeDtypeStruct((NF, 2 * XROWS, YROWS, LEV // 2), bf16),
        in_specs=[VMEM, VMEM],
        out_specs=HBM,
        scratch_shapes=[
            pltpu.VMEM((2, BLOCKS, NF, 4, YROWS, LEV // 2), bf16),
            pltpu.SemaphoreType.DMA((2, BLOCKS)),
        ],
        compiler_params=pltpu.CompilerParams(vmem_limit_bytes=24 * 2**20),
    )(packed, landed)


def shards(
    section_levels, to_cells, to_nodes, owner_map, forcing, vertical_map, coupling, relaxation
):
    derive, advance, edges = (jnp.asarray(c) for c in constants())
    operands = (
        section_levels, to_cells, jnp.swapaxes(to_nodes, 2, 3), owner_map.reshape(1, 64),
        forcing[0, 0], vertical_map, coupling, relaxation, derive, advance, edges,
    )
    packed, landed = main_call([
        pltpu.with_memory_space_constraint(x, pltpu.HBM) for x in operands
    ])
    return unpack_call(packed, landed)


def solution(mesh):
    in_specs = (
        P("grp", None, "gx", "gy", None),
        P("gx", "gy", None, None),
        P("gx", "gy", None, None),
        P("gx", "gy", None, None),
        P("gx", "gy", None, None, None),
        P(),
        P(),
        P(),
    )
    out_specs = P(None, "gx", "gy", "grp")
    return jax.shard_map(shards, mesh=mesh, in_specs=in_specs, out_specs=out_specs, check_vma=False)
```

```python
import functools

import jax
import jax.numpy as jnp
import numpy as np
from jax import lax
from jax.experimental import pallas as pl
from jax.experimental.pallas import tpu as pltpu
from jax.sharding import PartitionSpec as P

f32 = jnp.float32
bf16 = jnp.bfloat16
MESH = pl.DeviceIdType.MESH
HBM = pl.BlockSpec(memory_space=pltpu.HBM)
VMEM = pl.BlockSpec(memory_space=pltpu.VMEM)
SMEM = pl.BlockSpec(memory_space=pltpu.SMEM)

NF, NTEND, LEV = 10, 8, 128
PAIRS = NF // 2
XROWS, YROWS = 16, 32
BLOCKS = XROWS // 4
NODES = 4 * YROWS
CELLS = YROWS
CX, CZ, CY = 4, 8, 4
DT_DYN, DT_PHY = 0.1, 0.25


def gll_matrix():
    points = np.array([-1.0, -1.0 / np.sqrt(5.0), 1.0 / np.sqrt(5.0), 1.0])
    bary = np.ones(4)
    for i in range(4):
        for j in range(4):
            if i != j:
                bary[i] /= points[i] - points[j]
    matrix = np.zeros((4, 4))
    for i in range(4):
        for j in range(4):
            if i != j:
                matrix[i, j] = bary[j] / bary[i] / (points[i] - points[j])
        matrix[i, i] = -np.sum(matrix[i])
    return matrix


def constants():
    d = gll_matrix()
    weight1 = np.array([0.5, 1.0, 1.0, 0.5])
    weight = np.kron(weight1, np.tile(weight1, YROWS // 4))
    along_x = np.kron(d, np.eye(YROWS))
    along_y = np.kron(np.eye(4 * YROWS // 4), d)
    both = np.concatenate([along_x, along_y]) * (-DT_DYN * np.tile(weight, 2))[:, None]
    high = np.asarray(both, np.float32).astype(jnp.bfloat16)
    low = (both - high.astype(np.float64)).astype(np.float32).astype(jnp.bfloat16)
    derive = np.concatenate([high, low], axis=1)
    share = np.eye(YROWS)
    for y in range(3, YROWS - 1, 4):
        share[y, y + 1] = share[y + 1, y] = 1.0
    advance = np.zeros((BLOCKS, NODES, NODES + 2 * XROWS))
    for block in range(BLOCKS):
        advance[block, :, :NODES] = np.kron(np.eye(4), share)
        for i in range(4):
            advance[block, i * YROWS, NODES + 4 * block + i] = 1.0
            advance[block, i * YROWS + YROWS - 1, NODES + XROWS + 4 * block + i] = 1.0
    return derive, advance.astype(jnp.bfloat16)


def iota(shape, dim):
    return lax.broadcasted_iota(jnp.int32, shape, dim)


def halves(x):
    high = x.astype(bf16)
    return high, (x - high.astype(f32)).astype(bf16)


def mm(a, b):
    return jnp.dot(a, b, preferred_element_type=f32)


def mm_nt(a, b):
    return lax.dot_general(a, b, (((1,), (1,)), ((), ())), preferred_element_type=f32)


def mm2(a, b):
    high, low = halves(b)
    return mm(a, high) + mm(a, low)


def main_kernel(
    sec, tc, tn, own, frc, vmap, cpl, rel, derive_h, advance_h,
    packed, landed, given, chosen,
    cur, start, adv, advx, advd, wind, xfirst, xlast, xlo, xhi, yrow, ysend, ylo, yhi,
    csend, cgot, clo, chi, raw_first, raw_last,
    tc_v, tn_v, own_v, frc_v, v_v, rel_v, cpl_v, derive, advance,
    f2, ts, win, wgiven, vv, fa, fb1, fs2, fb2, cells, split, mixed, act, tend,
    small_sem, q_sem, s_send, s_recv, e_send, e_recv, c_send, c_recv, f_send, f_recv,
    o_send, o_recv,
):
    m, gx, gy = lax.axis_index("grp"), lax.axis_index("gx"), lax.axis_index("gy")
    z, x = gx // CX, gx % CX
    ngx = CX * CZ
    other = 1 - m
    partner = (other, gx, gy)
    left, right = (gx + ngx - 1) % ngx, (gx + 1) % ngx
    down, up = (gy + CY - 1) % CY, (gy + 1) % CY

    def plane_peer(j):
        return (1, z * CX + (x + j // CY) % CX, (gy + j % CY) % CY)

    def line_peer(member, j):
        return (member, ((z + j) % CZ) * CX + x, gy)

    barrier = pltpu.get_barrier_semaphore()

    def greet(peers):
        for peer in peers:
            pl.semaphore_signal(barrier, inc=1, device_id=peer, device_id_type=MESH)

    small = [
        pltpu.make_async_copy(src, dst, small_sem.at[k])
        for k, (src, dst) in enumerate([
            (frc, frc_v), (derive_h, derive), (advance_h, advance),
            (tc.at[pl.ds(m * BLOCKS, BLOCKS)], tc_v), (tn, tn_v),
            (own, own_v), (vmap, v_v), (rel, rel_v), (cpl, cpl_v),
        ])
    ]

    def current_in(block):
        rows = pl.ds(4 * block, 4)
        return pltpu.make_async_copy(sec.at[0, :, rows], cur.at[:, rows], q_sem.at[block])

    def row_of(member, turn):
        return (1 - member) * (BLOCKS - 1 - turn) + member * turn

    def start_in(turn):
        return pltpu.make_async_copy(
            sec.at[0, :, pl.ds(XROWS + 4 * turn, 4)], start.at[:, pl.ds(4 * turn, 4)],
            s_recv.at[turn],
        )

    def start_out(turn):
        rows = pl.ds(4 * (BLOCKS - 1 - turn), 4)
        return pltpu.make_async_remote_copy(
            sec.at[0, :, rows], start.at[:, rows], s_send.at[turn], s_recv.at[turn],
            device_id=partner, device_id_type=MESH,
        )

    def start_wait(turn):
        rows = start.at[:, pl.ds(4 * row_of(m, turn), 4)]
        pltpu.make_async_copy(rows, rows, s_recv.at[turn]).wait()

    def edge_copies(kinds):
        plan = [
            (adv.at[:, 0], xfirst, partner),
            (advx.at[:, XROWS - 1], xlast, partner),
            (csend, cgot, partner),
            (ysend.at[0, 0], yhi, (0, gx, down)),
            (ysend.at[0, 1], yhi, (1, gx, down)),
            (ysend.at[1, 0], ylo, (0, gx, up)),
            (ysend.at[1, 1], ylo, (1, gx, up)),
            (xfirst, xhi, (1, left, gy)),
            (xlast, xlo, (0, right, gy)),
        ]
        for block in range(BLOCKS):
            rows = pl.ds(4 * block, 4)
            plan.append((advx.at[:, rows], adv.at[:, rows], partner))
        return [
            pltpu.make_async_remote_copy(
                plan[k][0], plan[k][1], e_send.at[k], e_recv.at[k],
                device_id=plan[k][2], device_id_type=MESH,
            )
            for k in kinds
        ]

    def corner_copies(sides=(0, 1)):
        return [
            pltpu.make_async_remote_copy(
                cgot.at[2 * xs + ys], (chi, clo)[xs].at[1 - ys], c_send.at[2 * xs + ys],
                c_recv.at[2 * xs + ys],
                device_id=(1 - xs, (left, right)[xs], (down, up)[ys]), device_id_type=MESH,
            )
            for xs in sides for ys in range(2)
        ]

    def plane_copy(j, arriving):
        _, tx, ty = plane_peer(j)
        to = (tx % CX) * CY + ty
        me = x * CY + gy
        if arriving:
            me = ((x + CX - j // CY) % CX) * CY + (gy + CY - j % CY) % CY
        return pltpu.make_async_remote_copy(
            fa.at[pl.ds(pl.multiple_of(to * 8, 8), 8)],
            fb1.at[pl.ds(pl.multiple_of(me * 8, 8), 8)],
            f_send.at[0, j], f_recv.at[0, j], device_id=plane_peer(j), device_id_type=MESH,
        )

    def line_copy(member, j, arriving=False):
        to, me = (z + j) % CZ, z
        if arriving:
            me = (z + CZ - j) % CZ
        return pltpu.make_async_remote_copy(
            fs2.at[pl.ds(pl.multiple_of(to * 16, 16), 16)],
            fb2.at[pl.ds(pl.multiple_of(me * 16, 16), 16)],
            f_send.at[1 + member, j], f_recv.at[1, j],
            device_id=line_peer(member, j), device_id_type=MESH,
        )

    @pl.when(m == 0)
    def _():
        small[1].start()
        for block in ROWS:
            current_in(block).start()
        greet([partner, (0, gx, down), (0, gx, up)])
        greet([(1, left, gy), (1, left, down), (1, left, up)])
        greet([line_peer(1, j) for j in range(1, CZ)])
        for k, copy in enumerate(small):
            if k != 1:
                copy.start()
        small[1].wait()

        def put(p, row, value, raw):
            for k in range(2):
                part = value[:, k * LEV:(k + 1) * LEV]
                f = 2 * p + k
                if row < XROWS:
                    adv[f, row] = part.astype(bf16)
                else:
                    advx[f, row - XROWS] = part.astype(bf16)
                for side, edge in ((0, 0), (1, YROWS - 1)):
                    line = part[edge:edge + 1, :]
                    yrow[side, f, row:row + 1, :] = line
                    if raw is not None:
                        csend[2 * raw + side, f:f + 1, :] = line

        for turn, block in enumerate(ROWS):
            current_in(block).wait()
            for k in range(2):
                wind[k, block] = cur[k, 4 * block:4 * block + 4].reshape(NODES, LEV).astype(f32)
            for p in range(PAIRS):
                pair = [
                    cur[2 * p + k, 4 * block:4 * block + 4].reshape(NODES, LEV) for k in range(2)
                ]
                once = jnp.concatenate(pair, axis=1)
                slopes = mm(derive[...], jnp.concatenate([once, once], axis=0))
                u, v = wind[0, block], wind[1, block]
                value = jnp.concatenate([u, u], axis=1) * slopes[:NODES]
                value = value + jnp.concatenate([v, v], axis=1) * slopes[NODES:]
                first, last = value[:YROWS], value[3 * YROWS:]
                if block == 0:
                    put(p, 0, first, 0)
                elif block == 2 * BLOCKS - 1:
                    raw_first[p] = first
                    put(p, 4 * block + 3, last, 1)
                else:
                    shared = raw_last[p] + first
                    put(p, 4 * block - 1, shared, None)
                    put(p, 4 * block, shared, None)
                put(p, 4 * block + 1, value[YROWS:2 * YROWS], None)
                put(p, 4 * block + 2, value[2 * YROWS:3 * YROWS], None)
                if block == 2 * BLOCKS - 2:
                    shared = last + raw_first[p]
                    put(p, 4 * block + 3, shared, None)
                    put(p, 4 * block + 4, shared, None)
                elif block < 2 * BLOCKS - 2:
                    raw_last[p] = last
            if turn == 1:
                pl.semaphore_wait(barrier, 5)
                for copy in edge_copies((0, 1, 2)):
                    copy.start()
        for f in range(NF):
            for side in range(2):
                for half in range(2):
                    lines = yrow[side, f, half * XROWS:(half + 1) * XROWS]
                    ysend[side, half, f] = lines.astype(bf16)
        for copy in edge_copies((3, 4, 5, 6, 9, 10, 11, 12)):
            copy.start()
        xhi[...] = jnp.zeros_like(xhi)
        chi[...] = jnp.zeros_like(chi)

    @pl.when(m == 1)
    def _():
        small[0].start()
        greet([partner, (0, gx, down), (0, gx, up)])
        greet([(1, right, gy), (1, right, down), (1, right, up)])
        greet([plane_peer(j) for j in range(1, CX * CY)])
        greet([line_peer(1, j) for j in range(1, CZ)])
        for turn in range(BLOCKS):
            start_in(turn).start()
        for copy in small[1:]:
            copy.start()
        small[0].wait()
        for g in range(NTEND):
            f2[4 * g:4 * g + 4, :] = frc_v[g]
        source = iota((128, 256), 0)
        source = 2 * ((source % CZ) * (CX * CY) + source // CZ)
        slot = iota((128, 256), 1)
        rows_high, rows_low = halves(f2[...])
        empty = jnp.zeros((32, 256), bf16)
        total = jnp.zeros((128, 128), f32)
        for r in range(2):
            pick = (slot == source + r).astype(f32).astype(bf16)
            for part in (rows_high, rows_low):
                stack = [empty] * 4
                stack[r] = part
                total = total + mm_nt(pick, jnp.concatenate(stack, axis=0))
        fa[...] = total
        xlo[...] = jnp.zeros_like(xlo)
        clo[...] = jnp.zeros_like(clo)
        pl.semaphore_wait(barrier, 36)
        for j in range(1, CX * CY):
            plane_copy(j, False).start()
        for turn in range(BLOCKS):
            start_out(turn).start()
        mine = pl.ds(pl.multiple_of((x * CY + gy) * 8, 8), 8)
        fb1[mine, :] = fa[mine, :]

    def relay():
        for j in range(1, CX * CY):
            plane_copy(j, True).wait_recv()
        for k in range(CZ):
            fs2[16 * k:16 * k + 16, :] = fb1[pl.ds(k, 16, stride=CZ), :]
        for j in range(1, CZ):
            for member in range(2):
                line_copy(member, j).start()
        mine = pl.ds(pl.multiple_of(z * 16, 16), 16)
        pltpu.make_async_remote_copy(
            fs2.at[mine], fb2.at[mine], f_send.at[1, 0], f_recv.at[1, 0],
            device_id=partner, device_id_type=MESH,
        ).start()
        fb2[mine, :] = fs2[mine, :]

    for copy in small[3:]:
        copy.wait()
    spread = (iota((16, 128), 0) == (iota((16, 128), 1) // 32) * 4 + iota((16, 128), 1) % 4)
    spread = spread.astype(f32).astype(bf16)
    inside = (iota((128, 128), 0) // 4) % 8 == (iota((128, 128), 1) // 4) % 8
    for k in range(3):
        for block in range(BLOCKS):
            for ey in range(8):
                row = block * 32 + ey * 4
                one = tc_v[block, ey] if k == 0 else tn_v[block + BLOCKS * (k - 1), ey]
                ts[row:row + 4, :] = one.astype(f32)
        wide = jnp.where(inside, mm(ts[...].astype(bf16), spread), 0.0)
        if k == 0:
            for block in range(BLOCKS):
                win[block] = wide[32 * block:32 * block + 32].astype(bf16)
        else:
            turned = jnp.transpose(wide * DT_PHY)
            for block in range(BLOCKS):
                moved = turned if block == 0 else pltpu.roll(turned, 128 - 32 * block, 1)
                wgiven[block + BLOCKS * (k - 1)] = moved.astype(bf16)
    v_high, v_low = halves(v_v[...])
    vv[0:128, 0:128] = v_high
    vv[128:256, 0:128] = v_high
    vv[0:128, 128:256] = v_low
    vv[128:256, 128:256] = jnp.zeros((128, 128), bf16)

    owned = (iota((128, 64), 0) == own_v[...]).astype(f32)
    before = (iota((64, 64), 0) < iota((64, 64), 1)).astype(f32).astype(bf16)
    rank = mm(owned.astype(bf16), before)
    mine = (iota((256, 64), 1) == iota((256, 64), 0) // 4).astype(f32).astype(bf16)
    from0 = mm_nt(mine, jnp.where(rank < 0.5, owned, 0.0).astype(bf16)).astype(bf16)
    from1 = mm_nt(mine, jnp.where(rank < 0.5, 0.0, owned).astype(bf16)).astype(bf16)

    for g in range(NTEND):
        k, lane = iota((128, LEV), 0), iota((128, LEV), 1)
        chosen[g] = ((k % 32 // 4 == g) & (k // 64 == lane // 64)).astype(f32).astype(bf16)

    @pl.when(m == 0)
    def _():
        small[2].wait()
        small[0].wait()
        for copy in edge_copies((3, 5)):
            copy.wait_recv()

    @pl.when(m == 1)
    def _():
        small[1].wait()
        small[2].wait()
        for copy in edge_copies((0, 1, 2)):
            copy.wait_recv()
        for copy in edge_copies((7, 8)) + corner_copies():
            copy.start()
        relay()
        for copy in edge_copies((4, 6)):
            copy.wait_recv()

    lower = iota((YROWS, LEV), 1) < LEV // 2

    def pack(block, f, value):
        for i in range(2):
            a = value[i * YROWS:(i + 1) * YROWS]
            b = value[(i + 2) * YROWS:(i + 3) * YROWS]
            packed[0, block, f, i] = jnp.where(lower, a, pltpu.roll(b, 64, 1)).astype(bf16)
            packed[1, block, f, i] = jnp.where(lower, pltpu.roll(a, 64, 1), b).astype(bf16)

    def out_copy(turn, arriving=False):
        row = row_of(m, turn)
        return pltpu.make_async_remote_copy(
            packed.at[other, row], landed.at[row_of(other, turn) if arriving else row],
            o_send.at[turn], o_recv.at[turn], device_id=partner, device_id_type=MESH,
        )

    at = iota((XROWS, LEV), 0)

    for turn in range(BLOCKS):
        row = row_of(m, turn)
        final = turn == BLOCKS - 1
        start_wait(turn)

        @pl.when(m == 0)
        def _():
            if final:
                for copy in edge_copies((8,)) + corner_copies((1,)):
                    copy.wait_recv()

        @pl.when(m == 1)
        def _():
            edge_copies((9 + turn,))[0].wait_recv()
            if final:
                for copy in edge_copies((7,)) + corner_copies((0,)):
                    copy.wait_recv()

        weights = win[row]
        for p in range(PAIRS):
            parts, begun = [], []
            for k in range(2):
                f = 2 * p + k
                rows = [adv[f, 4 * row + i] for i in range(4)]
                halo = [ylo[f], yhi[f]]
                if final:
                    rows[0] = (rows[0].astype(f32) + xlo[f].astype(f32)).astype(bf16)
                    rows[3] = (rows[3].astype(f32) + xhi[f].astype(f32)).astype(bf16)
                    for side in range(2):
                        first = jnp.broadcast_to(clo[side, f:f + 1, :], (XROWS, LEV))
                        ending = jnp.broadcast_to(chi[side, f:f + 1, :], (XROWS, LEV))
                        extra = jnp.where(at == 0, first, jnp.where(at == XROWS - 1, ending, 0.0))
                        halo[side] = (halo[side].astype(f32) + extra).astype(bf16)
                parts.append(jnp.concatenate(rows + halo, axis=0))
                begun.append(start[f, pl.ds(4 * row, 4)].reshape(NODES, LEV).astype(f32))
            value = mm(advance[row], jnp.concatenate(parts, axis=1))
            value = (value + jnp.concatenate(begun, axis=1)).astype(bf16)
            got = mm(weights, value)
            for k in range(2):
                f = 2 * p + k
                advd[f, turn] = value[:, k * LEV:(k + 1) * LEV]
                one = got[:, k * LEV:(k + 1) * LEV]
                cells[turn, f] = one
                high, low = halves(one)
                split[turn, f, :, 0:LEV] = high
                split[turn, f, :, LEV:2 * LEV] = low
        got = mm(split[turn].reshape(NF * CELLS, 2 * LEV), vv[...])
        got = got[:, :LEV] + got[:, LEV:]
        warm = jnp.tanh(got)
        for f in range(NF):
            mixed[turn, f] = got[f * CELLS:(f + 1) * CELLS]
            act[turn, f] = warm[f * CELLS:(f + 1) * CELLS]
        for g in range(NTEND):
            acc = rel_v[g:g + 1, :] * (mixed[turn, g] - cells[turn, g])
            for f in range(NF):
                acc = acc + cpl_v[g, f] * act[turn, f]
            tend[turn, g] = acc.astype(bf16)
        for f in range(NTEND, NF):
            pack(row, f, advd[f, turn].astype(f32))
        weights = wgiven[m * BLOCKS + row][:, 0:CELLS]
        for p in range(NTEND // 2):
            pair = (2 * p, 2 * p + 1)
            value = mm(weights, jnp.concatenate([tend[turn, f] for f in pair], axis=1))
            for k, f in enumerate(pair):
                pack(row, f, value[:, k * LEV:(k + 1) * LEV] + advd[f, turn].astype(f32))
        out_copy(turn).start()

    @pl.when(m == 0)
    def _():
        for j in range(CZ):
            line_copy(0, j, True).wait_recv()

    @pl.when(m == 1)
    def _():
        for j in range(1, CZ):
            line_copy(1, j, True).wait_recv()

    table = fb2[...]
    lines = mm2(from0, table) + mm2(from1, pltpu.roll(table, 96, 1))
    lane = iota((256, 128), 1)
    lines = jnp.where((lane < 32) & (lane % 4 == iota((256, 128), 0) % 4), lines, 0.0)
    lines = lines + pltpu.roll(lines, 32, 1)
    lines = lines + pltpu.roll(lines, 64, 1)
    quarter = iota((2 * YROWS, LEV), 1) // 32
    for block in range(2 * BLOCKS):
        got = mm2(wgiven[block, :, 0:32], lines[32 * block:32 * block + 32])
        both = jnp.where(quarter < 2, got[:2 * YROWS], got[2 * YROWS:])
        high = both.astype(bf16).astype(f32)
        given[block] = jnp.where(quarter % 2 == 0, high, both - high).astype(bf16)

    @pl.when(m == 0)
    def _():
        for copy in edge_copies((0, 1, 2, 3, 4, 5, 6, 9, 10, 11, 12)):
            copy.wait_send()

    @pl.when(m == 1)
    def _():
        for turn in range(BLOCKS):
            start_out(turn).wait_send()
        for copy in edge_copies((7, 8)) + corner_copies():
            copy.wait_send()
        for j in range(1, CX * CY):
            plane_copy(j, False).wait_send()
        for j in range(1, CZ):
            for member in range(2):
                line_copy(member, j).wait_send()
        line_copy(0, 0).wait_send()

    for turn in range(BLOCKS):
        out_copy(turn).wait_send()
        out_copy(turn, True).wait_recv()


ROWS = (7, 0, 1, 2, 3, 4, 5, 6)


def main_call(args):
    v = pltpu.VMEM
    packed_shape = (BLOCKS, NF, 2, YROWS, LEV)
    dma = pltpu.SemaphoreType.DMA
    scratch = [
        v((NF, 2 * XROWS, YROWS, LEV), bf16),
        v((NF, XROWS, YROWS, LEV), bf16),
        v((NF, XROWS, YROWS, LEV), bf16),
        v((NF, XROWS, YROWS, LEV), bf16),
        v((NF, BLOCKS, NODES, LEV), bf16),
        v((2, 2 * BLOCKS, NODES, LEV), f32),
        v((NF, YROWS, LEV), bf16),
        v((NF, YROWS, LEV), bf16),
        v((NF, YROWS, LEV), bf16),
        v((NF, YROWS, LEV), bf16),
        v((2, NF, 2 * XROWS, LEV), f32),
        v((2, 2, NF, XROWS, LEV), bf16),
        v((NF, XROWS, LEV), bf16),
        v((NF, XROWS, LEV), bf16),
        v((4, 16, LEV), f32),
        v((4, 16, LEV), f32),
        v((2, 16, LEV), f32),
        v((2, 16, LEV), f32),
        v((PAIRS, YROWS, 2 * LEV), f32),
        v((PAIRS, YROWS, 2 * LEV), f32),
        v((BLOCKS, 8, 4, 16), bf16),
        v((2 * BLOCKS, 8, 4, 16), bf16),
        v((1, 64), jnp.int32),
        v((NTEND, 4, 256), f32),
        v((LEV, LEV), f32),
        v((NTEND, LEV), f32),
        pltpu.SMEM((NTEND, NF), f32),
        v((2 * NODES, 2 * NODES), bf16),
        v((BLOCKS, NODES, NODES + 2 * XROWS), bf16),
        v((32, 256), f32),
        v((128, 16), f32),
        v((BLOCKS, CELLS, 128), bf16),
        v((2 * BLOCKS, 128, 128), bf16),
        v((256, 256), bf16),
    ]
    scratch += [v((128, 128), f32)] * 4
    scratch += [
        v((BLOCKS, NF, CELLS, LEV), f32),
        v((BLOCKS, NF, CELLS, 2 * LEV), bf16),
        v((BLOCKS, NF, CELLS, LEV), f32),
        v((BLOCKS, NF, CELLS, LEV), f32),
        v((BLOCKS, NTEND, CELLS, LEV), bf16),
        dma((9,)), dma((2 * BLOCKS,)), dma((BLOCKS,)), dma((BLOCKS,)),
        dma((9 + BLOCKS,)), dma((9 + BLOCKS,)), dma((4,)), dma((4,)),
        dma((3, CX * CY)), dma((2, CX * CY)), dma((BLOCKS,)), dma((BLOCKS,)),
    ]
    return pl.pallas_call(
        main_kernel,
        out_shape=(
            jax.ShapeDtypeStruct((2,) + packed_shape, bf16),
            jax.ShapeDtypeStruct(packed_shape, bf16),
            jax.ShapeDtypeStruct((2 * BLOCKS, 2 * YROWS, LEV), bf16),
            jax.ShapeDtypeStruct((NTEND, 128, LEV), bf16),
        ),
        in_specs=[HBM] * 10,
        out_specs=(VMEM,) * 4,
        scratch_shapes=scratch,
        compiler_params=pltpu.CompilerParams(
            collective_id=0, has_side_effects=True, vmem_limit_bytes=40 * 2**20
        ),
    )(*args)


def unpack_kernel(packed, landed, given, chosen, out, stage, sems):
    m = lax.axis_index("grp")

    def copy(k, block):
        rows = (m if k == 0 else 1 - m) * XROWS + 4 * block
        return pltpu.make_async_copy(
            stage.at[k, block], out.at[:, pl.ds(rows, 4)], sems.at[k, block]
        )

    for k in range(2):
        for block in range(BLOCKS):
            lines = given[(m if k == 0 else 1 - m) * BLOCKS + block]
            for f in range(NF):
                if f < NTEND:
                    added = mm(lines, chosen[f])
                for i in range(2):
                    line = packed[m, block, f, i] if k == 0 else landed[block, f, i]
                    line = line.astype(f32)
                    if f < NTEND:
                        line = line + added[i * YROWS:(i + 1) * YROWS]
                    stage[k, block, f, i] = line[:, :LEV // 2].astype(bf16)
                    moved = pltpu.roll(line, 64, 1)
                    stage[k, block, f, i + 2] = moved[:, :LEV // 2].astype(bf16)
            copy(k, block).start()
    for k in range(2):
        for block in range(BLOCKS):
            copy(k, block).wait()


def unpack_call(*arrays):
    return pl.pallas_call(
        unpack_kernel,
        out_shape=jax.ShapeDtypeStruct((NF, 2 * XROWS, YROWS, LEV // 2), bf16),
        in_specs=[VMEM] * 4,
        out_specs=HBM,
        scratch_shapes=[
            pltpu.VMEM((2, BLOCKS, NF, 4, YROWS, LEV // 2), bf16),
            pltpu.SemaphoreType.DMA((2, BLOCKS)),
        ],
        compiler_params=pltpu.CompilerParams(vmem_limit_bytes=24 * 2**20),
    )(*arrays)


def shards(
    section_levels, to_cells, to_nodes, owner_map, forcing, vertical_map, coupling, relaxation
):
    derive, advance = (jnp.asarray(c) for c in constants())
    operands = (
        section_levels, to_cells, jnp.swapaxes(to_nodes, 2, 3), owner_map.reshape(1, 64),
        forcing[0, 0], vertical_map, coupling, relaxation, derive, advance,
    )
    results = main_call([
        pltpu.with_memory_space_constraint(x, pltpu.HBM) for x in operands
    ])
    return unpack_call(*results)


def solution(mesh):
    in_specs = (
        P("grp", None, "gx", "gy", None),
        P("gx", "gy", None, None),
        P("gx", "gy", None, None),
        P("gx", "gy", None, None),
        P("gx", "gy", None, None, None),
        P(),
        P(),
        P(),
    )
    out_specs = P(None, "gx", "gy", "grp")
    return jax.shard_map(shards, mesh=mesh, in_specs=in_specs, out_specs=out_specs, check_vma=False)
```

```python
import functools

import jax
import jax.numpy as jnp
import numpy as np
from jax import lax
from jax.experimental import pallas as pl
from jax.experimental.pallas import tpu as pltpu
from jax.sharding import PartitionSpec as P

f32 = jnp.float32
bf16 = jnp.bfloat16
MESH = pl.DeviceIdType.MESH
HBM = pl.BlockSpec(memory_space=pltpu.HBM)
VMEM = pl.BlockSpec(memory_space=pltpu.VMEM)
SMEM = pl.BlockSpec(memory_space=pltpu.SMEM)

NF, NTEND, LEV = 10, 8, 128
PAIRS = NF // 2
XROWS, YROWS = 16, 32
BLOCKS = XROWS // 4
NODES = 4 * YROWS
CELLS = YROWS
CX, CZ, CY = 4, 8, 4
DT_DYN, DT_PHY = 0.1, 0.25


def gll_matrix():
    points = np.array([-1.0, -1.0 / np.sqrt(5.0), 1.0 / np.sqrt(5.0), 1.0])
    bary = np.ones(4)
    for i in range(4):
        for j in range(4):
            if i != j:
                bary[i] /= points[i] - points[j]
    matrix = np.zeros((4, 4))
    for i in range(4):
        for j in range(4):
            if i != j:
                matrix[i, j] = bary[j] / bary[i] / (points[i] - points[j])
        matrix[i, i] = -np.sum(matrix[i])
    return matrix


def constants():
    d = gll_matrix()
    weight1 = np.array([0.5, 1.0, 1.0, 0.5])
    weight = np.kron(weight1, np.tile(weight1, YROWS // 4))
    along_x = np.kron(d, np.eye(YROWS))
    along_y = np.kron(np.eye(4 * YROWS // 4), d)
    both = np.concatenate([along_x, along_y]) * (-DT_DYN * np.tile(weight, 2))[:, None]
    high = np.asarray(both, np.float32).astype(jnp.bfloat16)
    low = (both - high.astype(np.float64)).astype(np.float32).astype(jnp.bfloat16)
    derive = np.concatenate([high, low], axis=1)
    share = np.eye(YROWS)
    for y in range(3, YROWS - 1, 4):
        share[y, y + 1] = share[y + 1, y] = 1.0
    advance = np.zeros((BLOCKS, NODES, NODES + 2 * XROWS))
    for block in range(BLOCKS):
        advance[block, :, :NODES] = np.kron(np.eye(4), share)
        for i in range(4):
            advance[block, i * YROWS, NODES + 4 * block + i] = 1.0
            advance[block, i * YROWS + YROWS - 1, NODES + XROWS + 4 * block + i] = 1.0
    return derive, advance.astype(jnp.bfloat16)


def iota(shape, dim):
    return lax.broadcasted_iota(jnp.int32, shape, dim)


def halves(x):
    high = x.astype(bf16)
    return high, (x - high.astype(f32)).astype(bf16)


def mm(a, b):
    return jnp.dot(a, b, preferred_element_type=f32)


def mm_nt(a, b):
    return lax.dot_general(a, b, (((1,), (1,)), ((), ())), preferred_element_type=f32)


def mm2(a, b):
    high, low = halves(b)
    return mm(a, high) + mm(a, low)


def main_kernel(
    sec, tc, tn, own, frc, vmap, cpl, rel, derive_h, advance_h,
    packed, landed, given, chosen,
    cur, start, adv, advx, advd, wind, xfirst, xlast, xlo, xhi, yrow, ysend, ylo, yhi,
    csend, cgot, clo, chi, raw_first, raw_last,
    tc_v, tn_v, own_v, frc_v, v_v, rel_v, cpl_v, derive, advance,
    f2, ts, win, wgiven, vv, fa, fb1, fs2, fb2, cells, split, mixed, act, tend,
    small_sem, q_sem, s_send, s_recv, e_send, e_recv, c_send, c_recv, f_send, f_recv,
    o_send, o_recv,
):
    m, gx, gy = lax.axis_index("grp"), lax.axis_index("gx"), lax.axis_index("gy")
    z, x = gx // CX, gx % CX
    ngx = CX * CZ
    other = 1 - m
    partner = (other, gx, gy)
    left, right = (gx + ngx - 1) % ngx, (gx + 1) % ngx
    down, up = (gy + CY - 1) % CY, (gy + 1) % CY

    def plane_peer(j):
        return (1, z * CX + (x + j // CY) % CX, (gy + j % CY) % CY)

    def line_peer(j):
        return (1, ((z + j) % CZ) * CX + x, gy)

    barrier = pltpu.get_barrier_semaphore()

    def greet(peers):
        for peer in peers:
            pl.semaphore_signal(barrier, inc=1, device_id=peer, device_id_type=MESH)

    small = [
        pltpu.make_async_copy(src, dst, small_sem.at[k])
        for k, (src, dst) in enumerate([
            (frc, frc_v), (derive_h, derive), (advance_h, advance),
            (tc.at[pl.ds(m * BLOCKS, BLOCKS)], tc_v), (tn, tn_v),
            (own, own_v), (vmap, v_v), (rel, rel_v), (cpl, cpl_v),
        ])
    ]

    def current_in(block):
        rows = pl.ds(4 * block, 4)
        return pltpu.make_async_copy(sec.at[0, :, rows], cur.at[:, rows], q_sem.at[block])

    def row_of(member, turn):
        return (1 - member) * (BLOCKS - 1 - turn) + member * turn

    def start_in(turn):
        return pltpu.make_async_copy(
            sec.at[0, :, pl.ds(XROWS + 4 * turn, 4)], start.at[:, pl.ds(4 * turn, 4)],
            s_recv.at[turn],
        )

    def start_out(turn):
        rows = pl.ds(4 * (BLOCKS - 1 - turn), 4)
        return pltpu.make_async_remote_copy(
            sec.at[0, :, rows], start.at[:, rows], s_send.at[turn], s_recv.at[turn],
            device_id=partner, device_id_type=MESH,
        )

    def start_wait(turn):
        rows = start.at[:, pl.ds(4 * row_of(m, turn), 4)]
        pltpu.make_async_copy(rows, rows, s_recv.at[turn]).wait()

    def edge_copies(kinds):
        plan = [
            (adv.at[:, 0], xfirst, partner),
            (advx.at[:, XROWS - 1], xlast, partner),
            (csend, cgot, partner),
            (ysend.at[0, 0], yhi, (0, gx, down)),
            (ysend.at[0, 1], yhi, (1, gx, down)),
            (ysend.at[1, 0], ylo, (0, gx, up)),
            (ysend.at[1, 1], ylo, (1, gx, up)),
            (xfirst, xhi, (1, left, gy)),
            (xlast, xlo, (0, right, gy)),
        ]
        for block in range(BLOCKS):
            rows = pl.ds(4 * block, 4)
            plan.append((advx.at[:, rows], adv.at[:, rows], partner))
        return [
            pltpu.make_async_remote_copy(
                plan[k][0], plan[k][1], e_send.at[k], e_recv.at[k],
                device_id=plan[k][2], device_id_type=MESH,
            )
            for k in kinds
        ]

    def corner_copies(sides=(0, 1)):
        return [
            pltpu.make_async_remote_copy(
                cgot.at[2 * xs + ys], (chi, clo)[xs].at[1 - ys], c_send.at[2 * xs + ys],
                c_recv.at[2 * xs + ys],
                device_id=(1 - xs, (left, right)[xs], (down, up)[ys]), device_id_type=MESH,
            )
            for xs in sides for ys in range(2)
        ]

    def plane_copy(j, arriving):
        _, tx, ty = plane_peer(j)
        to = (tx % CX) * CY + ty
        me = x * CY + gy
        if arriving:
            me = ((x + CX - j // CY) % CX) * CY + (gy + CY - j % CY) % CY
        return pltpu.make_async_remote_copy(
            fa.at[pl.ds(pl.multiple_of(to * 8, 8), 8)],
            fb1.at[pl.ds(pl.multiple_of(me * 8, 8), 8)],
            f_send.at[0, j], f_recv.at[0, j], device_id=plane_peer(j), device_id_type=MESH,
        )

    def line_copy(j, arriving=False):
        to, me = (z + j) % CZ, z
        if arriving:
            me = (z + CZ - j) % CZ
        return pltpu.make_async_remote_copy(
            fs2.at[pl.ds(pl.multiple_of(to * 16, 16), 16)],
            fb2.at[pl.ds(pl.multiple_of(me * 16, 16), 16)],
            f_send.at[1, j], f_recv.at[1, j], device_id=line_peer(j), device_id_type=MESH,
        )

    def table_copy():
        return pltpu.make_async_remote_copy(
            fb2, fb2, f_send.at[1, 0], f_recv.at[1, 0], device_id=partner, device_id_type=MESH
        )

    @pl.when(m == 0)
    def _():
        small[1].start()
        for block in ROWS:
            current_in(block).start()
        greet([partner, (0, gx, down), (0, gx, up)])
        greet([(1, left, gy), (1, left, down), (1, left, up)])
        for k, copy in enumerate(small):
            if k != 1:
                copy.start()
        small[1].wait()

        def put(p, row, value, raw):
            for k in range(2):
                part = value[:, k * LEV:(k + 1) * LEV]
                f = 2 * p + k
                if row < XROWS:
                    adv[f, row] = part.astype(bf16)
                else:
                    advx[f, row - XROWS] = part.astype(bf16)
                for side, edge in ((0, 0), (1, YROWS - 1)):
                    line = part[edge:edge + 1, :]
                    yrow[side, f, row:row + 1, :] = line
                    if raw is not None:
                        csend[2 * raw + side, f:f + 1, :] = line

        for turn, block in enumerate(ROWS):
            current_in(block).wait()
            for k in range(2):
                wind[k, block] = cur[k, 4 * block:4 * block + 4].reshape(NODES, LEV).astype(f32)
            for p in range(PAIRS):
                pair = [
                    cur[2 * p + k, 4 * block:4 * block + 4].reshape(NODES, LEV) for k in range(2)
                ]
                once = jnp.concatenate(pair, axis=1)
                slopes = mm(derive[...], jnp.concatenate([once, once], axis=0))
                u, v = wind[0, block], wind[1, block]
                value = jnp.concatenate([u, u], axis=1) * slopes[:NODES]
                value = value + jnp.concatenate([v, v], axis=1) * slopes[NODES:]
                first, last = value[:YROWS], value[3 * YROWS:]
                if block == 0:
                    put(p, 0, first, 0)
                elif block == 2 * BLOCKS - 1:
                    raw_first[p] = first
                    put(p, 4 * block + 3, last, 1)
                else:
                    shared = raw_last[p] + first
                    put(p, 4 * block - 1, shared, None)
                    put(p, 4 * block, shared, None)
                put(p, 4 * block + 1, value[YROWS:2 * YROWS], None)
                put(p, 4 * block + 2, value[2 * YROWS:3 * YROWS], None)
                if block == 2 * BLOCKS - 2:
                    shared = last + raw_first[p]
                    put(p, 4 * block + 3, shared, None)
                    put(p, 4 * block + 4, shared, None)
                elif block < 2 * BLOCKS - 2:
                    raw_last[p] = last
            if turn == 1:
                pl.semaphore_wait(barrier, 5)
                for copy in edge_copies((0, 1, 2)):
                    copy.start()
        for f in range(NF):
            for side in range(2):
                for half in range(2):
                    lines = yrow[side, f, half * XROWS:(half + 1) * XROWS]
                    ysend[side, half, f] = lines.astype(bf16)
        for copy in edge_copies((3, 4, 5, 6, 9, 10, 11, 12)):
            copy.start()
        xhi[...] = jnp.zeros_like(xhi)
        chi[...] = jnp.zeros_like(chi)

    @pl.when(m == 1)
    def _():
        small[0].start()
        greet([plane_peer(j) for j in PLANE])
        greet([line_peer(j) for j in LINE])
        greet([(1, right, gy), (1, right, down), (1, right, up)])
        greet([partner, (0, gx, down), (0, gx, up)])
        for turn in range(BLOCKS):
            start_in(turn).start()
        for copy in small[1:]:
            copy.start()
        small[0].wait()
        for g in range(NTEND):
            f2[4 * g:4 * g + 4, :] = frc_v[g]
        source = iota((128, 256), 0)
        source = 2 * ((source % CZ) * (CX * CY) + source // CZ)
        slot = iota((128, 256), 1)
        rows_high, rows_low = halves(f2[...])
        empty = jnp.zeros((32, 256), bf16)
        total = jnp.zeros((128, 128), f32)
        for r in range(2):
            pick = (slot == source + r).astype(f32).astype(bf16)
            for part in (rows_high, rows_low):
                stack = [empty] * 4
                stack[r] = part
                total = total + mm_nt(pick, jnp.concatenate(stack, axis=0))
        fa[...] = total
        xlo[...] = jnp.zeros_like(xlo)
        clo[...] = jnp.zeros_like(clo)
        pl.semaphore_wait(barrier, 29)
        for j in PLANE:
            plane_copy(j, False).start()
        for turn in range(BLOCKS):
            start_out(turn).start()
        for copy in edge_copies((0, 1, 2)):
            copy.wait_recv()
        for copy in edge_copies((7, 8)) + corner_copies():
            copy.start()
        mine = pl.ds(pl.multiple_of((x * CY + gy) * 8, 8), 8)
        fb1[mine, :] = fa[mine, :]

    def relay():
        for j in range(1, CX * CY):
            plane_copy(j, True).wait_recv()
        for k in range(CZ):
            fs2[16 * k:16 * k + 16, :] = fb1[pl.ds(k, 16, stride=CZ), :]
        for j in LINE:
            line_copy(j).start()
        mine = pl.ds(pl.multiple_of(z * 16, 16), 16)
        fb2[mine, :] = fs2[mine, :]

    for copy in small[3:]:
        copy.wait()
    spread = (iota((16, 128), 0) == (iota((16, 128), 1) // 32) * 4 + iota((16, 128), 1) % 4)
    spread = spread.astype(f32).astype(bf16)
    inside = (iota((128, 128), 0) // 4) % 8 == (iota((128, 128), 1) // 4) % 8
    for k in range(3):
        for block in range(BLOCKS):
            for ey in range(8):
                row = block * 32 + ey * 4
                one = tc_v[block, ey] if k == 0 else tn_v[block + BLOCKS * (k - 1), ey]
                ts[row:row + 4, :] = one.astype(f32)
        wide = jnp.where(inside, mm(ts[...].astype(bf16), spread), 0.0)
        if k == 0:
            for block in range(BLOCKS):
                win[block] = wide[32 * block:32 * block + 32].astype(bf16)
        else:
            turned = jnp.transpose(wide * DT_PHY)
            for block in range(BLOCKS):
                moved = turned if block == 0 else pltpu.roll(turned, 128 - 32 * block, 1)
                wgiven[block + BLOCKS * (k - 1)] = moved.astype(bf16)
    v_high, v_low = halves(v_v[...])
    vv[0:128, 0:128] = v_high
    vv[128:256, 0:128] = v_high
    vv[0:128, 128:256] = v_low
    vv[128:256, 128:256] = jnp.zeros((128, 128), bf16)

    owned = (iota((128, 64), 0) == own_v[...]).astype(f32)
    before = (iota((64, 64), 0) < iota((64, 64), 1)).astype(f32).astype(bf16)
    rank = mm(owned.astype(bf16), before)
    mine = (iota((256, 64), 1) == iota((256, 64), 0) // 4).astype(f32).astype(bf16)
    from0 = mm_nt(mine, jnp.where(rank < 0.5, owned, 0.0).astype(bf16)).astype(bf16)
    from1 = mm_nt(mine, jnp.where(rank < 0.5, 0.0, owned).astype(bf16)).astype(bf16)

    for g in range(NTEND):
        k, lane = iota((128, LEV), 0), iota((128, LEV), 1)
        chosen[g] = ((k % 32 // 4 == g) & (k // 64 == lane // 64)).astype(f32).astype(bf16)

    @pl.when(m == 0)
    def _():
        small[2].wait()
        small[0].wait()
        for copy in edge_copies((3, 5)):
            copy.wait_recv()

    @pl.when(m == 1)
    def _():
        small[1].wait()
        small[2].wait()
        relay()
        for copy in edge_copies((4, 6)):
            copy.wait_recv()

    lower = iota((YROWS, LEV), 1) < LEV // 2

    def pack(block, f, value):
        for i in range(2):
            a = value[i * YROWS:(i + 1) * YROWS]
            b = value[(i + 2) * YROWS:(i + 3) * YROWS]
            packed[0, block, f, i] = jnp.where(lower, a, pltpu.roll(b, 64, 1)).astype(bf16)
            packed[1, block, f, i] = jnp.where(lower, pltpu.roll(a, 64, 1), b).astype(bf16)

    def out_copy(turn, arriving=False):
        row = row_of(m, turn)
        return pltpu.make_async_remote_copy(
            packed.at[other, row], landed.at[row_of(other, turn) if arriving else row],
            o_send.at[turn], o_recv.at[turn], device_id=partner, device_id_type=MESH,
        )

    at = iota((XROWS, LEV), 0)

    for turn in range(BLOCKS):
        row = row_of(m, turn)
        final = turn == BLOCKS - 1
        start_wait(turn)

        @pl.when(m == 0)
        def _():
            if final:
                for copy in edge_copies((8,)) + corner_copies((1,)):
                    copy.wait_recv()

        @pl.when(m == 1)
        def _():
            edge_copies((9 + turn,))[0].wait_recv()
            if final:
                for copy in edge_copies((7,)) + corner_copies((0,)):
                    copy.wait_recv()

        weights = win[row]
        for p in range(PAIRS):
            parts, begun = [], []
            for k in range(2):
                f = 2 * p + k
                rows = [adv[f, 4 * row + i] for i in range(4)]
                halo = [ylo[f], yhi[f]]
                if final:
                    rows[0] = (rows[0].astype(f32) + xlo[f].astype(f32)).astype(bf16)
                    rows[3] = (rows[3].astype(f32) + xhi[f].astype(f32)).astype(bf16)
                    for side in range(2):
                        first = jnp.broadcast_to(clo[side, f:f + 1, :], (XROWS, LEV))
                        ending = jnp.broadcast_to(chi[side, f:f + 1, :], (XROWS, LEV))
                        extra = jnp.where(at == 0, first, jnp.where(at == XROWS - 1, ending, 0.0))
                        halo[side] = (halo[side].astype(f32) + extra).astype(bf16)
                parts.append(jnp.concatenate(rows + halo, axis=0))
                begun.append(start[f, pl.ds(4 * row, 4)].reshape(NODES, LEV).astype(f32))
            value = mm(advance[row], jnp.concatenate(parts, axis=1))
            value = (value + jnp.concatenate(begun, axis=1)).astype(bf16)
            got = mm(weights, value)
            for k in range(2):
                f = 2 * p + k
                advd[f, turn] = value[:, k * LEV:(k + 1) * LEV]
                one = got[:, k * LEV:(k + 1) * LEV]
                cells[turn, f] = one
                high, low = halves(one)
                split[turn, f, :, 0:LEV] = high
                split[turn, f, :, LEV:2 * LEV] = low
        got = mm(split[turn].reshape(NF * CELLS, 2 * LEV), vv[...])
        got = got[:, :LEV] + got[:, LEV:]
        warm = jnp.tanh(got)
        for f in range(NF):
            mixed[turn, f] = got[f * CELLS:(f + 1) * CELLS]
            act[turn, f] = warm[f * CELLS:(f + 1) * CELLS]
        for g in range(NTEND):
            acc = rel_v[g:g + 1, :] * (mixed[turn, g] - cells[turn, g])
            for f in range(NF):
                acc = acc + cpl_v[g, f] * act[turn, f]
            tend[turn, g] = acc.astype(bf16)
        for f in range(NTEND, NF):
            pack(row, f, advd[f, turn].astype(f32))
        weights = wgiven[m * BLOCKS + row][:, 0:CELLS]
        for p in range(NTEND // 2):
            pair = (2 * p, 2 * p + 1)
            value = mm(weights, jnp.concatenate([tend[turn, f] for f in pair], axis=1))
            for k, f in enumerate(pair):
                pack(row, f, value[:, k * LEV:(k + 1) * LEV] + advd[f, turn].astype(f32))
        out_copy(turn).start()

    @pl.when(m == 0)
    def _():
        table_copy().wait_recv()

    @pl.when(m == 1)
    def _():
        for j in range(1, CZ):
            line_copy(j, True).wait_recv()
        table_copy().start()

    table = fb2[...]
    lines = mm2(from0, table) + mm2(from1, pltpu.roll(table, 96, 1))
    lane = iota((256, 128), 1)
    lines = jnp.where((lane < 32) & (lane % 4 == iota((256, 128), 0) % 4), lines, 0.0)
    lines = lines + pltpu.roll(lines, 32, 1)
    lines = lines + pltpu.roll(lines, 64, 1)
    quarter = iota((2 * YROWS, LEV), 1) // 32
    for block in range(2 * BLOCKS):
        got = mm2(wgiven[block, :, 0:32], lines[32 * block:32 * block + 32])
        both = jnp.where(quarter < 2, got[:2 * YROWS], got[2 * YROWS:])
        high = both.astype(bf16).astype(f32)
        given[block] = jnp.where(quarter % 2 == 0, high, both - high).astype(bf16)

    @pl.when(m == 0)
    def _():
        for copy in edge_copies((0, 1, 2, 3, 4, 5, 6, 9, 10, 11, 12)):
            copy.wait_send()

    @pl.when(m == 1)
    def _():
        for turn in range(BLOCKS):
            start_out(turn).wait_send()
        for copy in edge_copies((7, 8)) + corner_copies():
            copy.wait_send()
        for j in range(1, CX * CY):
            plane_copy(j, False).wait_send()
        for j in range(1, CZ):
            line_copy(j).wait_send()
        table_copy().wait_send()

    for turn in range(BLOCKS):
        out_copy(turn).wait_send()
        out_copy(turn, True).wait_recv()


ROWS = (7, 0, 1, 2, 3, 4, 5, 6)


def hops_to(j, count):
    return min(j % count, count - j % count)


PLANE = sorted(range(1, CX * CY), key=lambda j: -hops_to(j // CY, CX) - hops_to(j, CY))
LINE = sorted(range(1, CZ), key=lambda j: -hops_to(j, CZ))


def main_call(args):
    v = pltpu.VMEM
    packed_shape = (BLOCKS, NF, 2, YROWS, LEV)
    dma = pltpu.SemaphoreType.DMA
    scratch = [
        v((NF, 2 * XROWS, YROWS, LEV), bf16),
        v((NF, XROWS, YROWS, LEV), bf16),
        v((NF, XROWS, YROWS, LEV), bf16),
        v((NF, XROWS, YROWS, LEV), bf16),
        v((NF, BLOCKS, NODES, LEV), bf16),
        v((2, 2 * BLOCKS, NODES, LEV), f32),
        v((NF, YROWS, LEV), bf16),
        v((NF, YROWS, LEV), bf16),
        v((NF, YROWS, LEV), bf16),
        v((NF, YROWS, LEV), bf16),
        v((2, NF, 2 * XROWS, LEV), f32),
        v((2, 2, NF, XROWS, LEV), bf16),
        v((NF, XROWS, LEV), bf16),
        v((NF, XROWS, LEV), bf16),
        v((4, 16, LEV), f32),
        v((4, 16, LEV), f32),
        v((2, 16, LEV), f32),
        v((2, 16, LEV), f32),
        v((PAIRS, YROWS, 2 * LEV), f32),
        v((PAIRS, YROWS, 2 * LEV), f32),
        v((BLOCKS, 8, 4, 16), bf16),
        v((2 * BLOCKS, 8, 4, 16), bf16),
        v((1, 64), jnp.int32),
        v((NTEND, 4, 256), f32),
        v((LEV, LEV), f32),
        v((NTEND, LEV), f32),
        pltpu.SMEM((NTEND, NF), f32),
        v((2 * NODES, 2 * NODES), bf16),
        v((BLOCKS, NODES, NODES + 2 * XROWS), bf16),
        v((32, 256), f32),
        v((128, 16), f32),
        v((BLOCKS, CELLS, 128), bf16),
        v((2 * BLOCKS, 128, 128), bf16),
        v((256, 256), bf16),
    ]
    scratch += [v((128, 128), f32)] * 4
    scratch += [
        v((BLOCKS, NF, CELLS, LEV), f32),
        v((BLOCKS, NF, CELLS, 2 * LEV), bf16),
        v((BLOCKS, NF, CELLS, LEV), f32),
        v((BLOCKS, NF, CELLS, LEV), f32),
        v((BLOCKS, NTEND, CELLS, LEV), bf16),
        dma((9,)), dma((2 * BLOCKS,)), dma((BLOCKS,)), dma((BLOCKS,)),
        dma((9 + BLOCKS,)), dma((9 + BLOCKS,)), dma((4,)), dma((4,)),
        dma((2, CX * CY)), dma((2, CX * CY)), dma((BLOCKS,)), dma((BLOCKS,)),
    ]
    return pl.pallas_call(
        main_kernel,
        out_shape=(
            jax.ShapeDtypeStruct((2,) + packed_shape, bf16),
            jax.ShapeDtypeStruct(packed_shape, bf16),
            jax.ShapeDtypeStruct((2 * BLOCKS, 2 * YROWS, LEV), bf16),
            jax.ShapeDtypeStruct((NTEND, 128, LEV), bf16),
        ),
        in_specs=[HBM] * 10,
        out_specs=(VMEM,) * 4,
        scratch_shapes=scratch,
        compiler_params=pltpu.CompilerParams(
            collective_id=0, has_side_effects=True, vmem_limit_bytes=40 * 2**20
        ),
    )(*args)


def unpack_kernel(packed, landed, given, chosen, out, stage, sems):
    m = lax.axis_index("grp")

    def copy(k, block):
        rows = (m if k == 0 else 1 - m) * XROWS + 4 * block
        return pltpu.make_async_copy(
            stage.at[k, block], out.at[:, pl.ds(rows, 4)], sems.at[k, block]
        )

    for k in range(2):
        for block in range(BLOCKS):
            lines = given[(m if k == 0 else 1 - m) * BLOCKS + block]
            for f in range(NF):
                if f < NTEND:
                    added = mm(lines, chosen[f])
                for i in range(2):
                    line = packed[m, block, f, i] if k == 0 else landed[block, f, i]
                    line = line.astype(f32)
                    if f < NTEND:
                        line = line + added[i * YROWS:(i + 1) * YROWS]
                    stage[k, block, f, i] = line[:, :LEV // 2].astype(bf16)
                    moved = pltpu.roll(line, 64, 1)
                    stage[k, block, f, i + 2] = moved[:, :LEV // 2].astype(bf16)
            copy(k, block).start()
    for k in range(2):
        for block in range(BLOCKS):
            copy(k, block).wait()


def unpack_call(*arrays):
    return pl.pallas_call(
        unpack_kernel,
        out_shape=jax.ShapeDtypeStruct((NF, 2 * XROWS, YROWS, LEV // 2), bf16),
        in_specs=[VMEM] * 4,
        out_specs=HBM,
        scratch_shapes=[
            pltpu.VMEM((2, BLOCKS, NF, 4, YROWS, LEV // 2), bf16),
            pltpu.SemaphoreType.DMA((2, BLOCKS)),
        ],
        compiler_params=pltpu.CompilerParams(vmem_limit_bytes=24 * 2**20),
    )(*arrays)


def shards(
    section_levels, to_cells, to_nodes, owner_map, forcing, vertical_map, coupling, relaxation
):
    derive, advance = (jnp.asarray(c) for c in constants())
    operands = (
        section_levels, to_cells, jnp.swapaxes(to_nodes, 2, 3), owner_map.reshape(1, 64),
        forcing[0, 0], vertical_map, coupling, relaxation, derive, advance,
    )
    results = main_call([
        pltpu.with_memory_space_constraint(x, pltpu.HBM) for x in operands
    ])
    return unpack_call(*results)


def solution(mesh):
    in_specs = (
        P("grp", None, "gx", "gy", None),
        P("gx", "gy", None, None),
        P("gx", "gy", None, None),
        P("gx", "gy", None, None),
        P("gx", "gy", None, None, None),
        P(),
        P(),
        P(),
    )
    out_specs = P(None, "gx", "gy", "grp")
    return jax.shard_map(shards, mesh=mesh, in_specs=in_specs, out_specs=out_specs, check_vma=False)
```

```python
import functools

import jax
import jax.numpy as jnp
import numpy as np
from jax import lax
from jax.experimental import pallas as pl
from jax.experimental.pallas import tpu as pltpu
from jax.sharding import PartitionSpec as P

f32 = jnp.float32
bf16 = jnp.bfloat16
MESH = pl.DeviceIdType.MESH
HBM = pl.BlockSpec(memory_space=pltpu.HBM)
VMEM = pl.BlockSpec(memory_space=pltpu.VMEM)
SMEM = pl.BlockSpec(memory_space=pltpu.SMEM)

NF, NTEND, LEV = 10, 8, 128
PAIRS = NF // 2
XROWS, YROWS = 16, 32
BLOCKS = XROWS // 4
NODES = 4 * YROWS
CELLS = YROWS
CX, CZ, CY = 4, 8, 4
DT_DYN, DT_PHY = 0.1, 0.25


def gll_matrix():
    points = np.array([-1.0, -1.0 / np.sqrt(5.0), 1.0 / np.sqrt(5.0), 1.0])
    bary = np.ones(4)
    for i in range(4):
        for j in range(4):
            if i != j:
                bary[i] /= points[i] - points[j]
    matrix = np.zeros((4, 4))
    for i in range(4):
        for j in range(4):
            if i != j:
                matrix[i, j] = bary[j] / bary[i] / (points[i] - points[j])
        matrix[i, i] = -np.sum(matrix[i])
    return matrix


def constants():
    d = gll_matrix()
    weight1 = np.array([0.5, 1.0, 1.0, 0.5])
    weight = np.kron(weight1, np.tile(weight1, YROWS // 4))
    along_x = np.kron(d, np.eye(YROWS))
    along_y = np.kron(np.eye(4 * YROWS // 4), d)
    both = np.concatenate([along_x, along_y]) * (-DT_DYN * np.tile(weight, 2))[:, None]
    high = np.asarray(both, np.float32).astype(jnp.bfloat16)
    low = (both - high.astype(np.float64)).astype(np.float32).astype(jnp.bfloat16)
    derive = np.concatenate([high, low], axis=1)
    share = np.eye(YROWS)
    for y in range(3, YROWS - 1, 4):
        share[y, y + 1] = share[y + 1, y] = 1.0
    advance = np.zeros((BLOCKS, NODES, NODES + 2 * XROWS))
    for block in range(BLOCKS):
        advance[block, :, :NODES] = np.kron(np.eye(4), share)
        for i in range(4):
            advance[block, i * YROWS, NODES + 4 * block + i] = 1.0
            advance[block, i * YROWS + YROWS - 1, NODES + XROWS + 4 * block + i] = 1.0
    return derive, advance.astype(jnp.bfloat16)


def iota(shape, dim):
    return lax.broadcasted_iota(jnp.int32, shape, dim)


def halves(x):
    high = x.astype(bf16)
    return high, (x - high.astype(f32)).astype(bf16)


def mm(a, b):
    return jnp.dot(a, b, preferred_element_type=f32)


def mm_nt(a, b):
    return lax.dot_general(a, b, (((1,), (1,)), ((), ())), preferred_element_type=f32)


def mm2(a, b):
    high, low = halves(b)
    return mm(a, high) + mm(a, low)


def main_kernel(
    sec, tc, tn, own, frc, vmap, cpl, rel, derive_h, advance_h,
    packed, landed, given, chosen,
    cur, start, adv, advx, advd, wind, xfirst, xlast, xlo, xhi, yrow, ysend, ylo, yhi,
    csend, cgot, clo, chi, raw_first, raw_last,
    tc_v, tn_v, own_v, frc_v, v_v, rel_v, cpl_v, derive, advance,
    f2, ts, win, wgiven, vv, fa, fb1, fs2, fb2, cells, split, mixed, act, tend,
    small_sem, q_sem, s_send, s_recv, e_send, e_recv, c_send, c_recv, f_send, f_recv,
    o_send, o_recv,
):
    m, gx, gy = lax.axis_index("grp"), lax.axis_index("gx"), lax.axis_index("gy")
    z, x = gx // CX, gx % CX
    ngx = CX * CZ
    other = 1 - m
    partner = (other, gx, gy)
    left, right = (gx + ngx - 1) % ngx, (gx + 1) % ngx
    down, up = (gy + CY - 1) % CY, (gy + 1) % CY

    def plane_peer(j):
        return (1, z * CX + (x + j // CY) % CX, (gy + j % CY) % CY)

    def line_peer(j):
        return (1, ((z + j) % CZ) * CX + x, gy)

    barrier = pltpu.get_barrier_semaphore()

    def greet(peers):
        for peer in peers:
            pl.semaphore_signal(barrier, inc=1, device_id=peer, device_id_type=MESH)

    small = [
        pltpu.make_async_copy(src, dst, small_sem.at[k])
        for k, (src, dst) in enumerate([
            (frc, frc_v), (derive_h, derive), (advance_h, advance),
            (tc.at[pl.ds(m * BLOCKS, BLOCKS)], tc_v), (tn, tn_v),
            (own, own_v), (vmap, v_v), (rel, rel_v), (cpl, cpl_v),
        ])
    ]

    def current_in(block):
        rows = pl.ds(4 * block, 4)
        return pltpu.make_async_copy(sec.at[0, :, rows], cur.at[:, rows], q_sem.at[block])

    def row_of(member, turn):
        return (1 - member) * (BLOCKS - 1 - turn) + member * turn

    def start_in(turn):
        return pltpu.make_async_copy(
            sec.at[0, :, pl.ds(XROWS + 4 * turn, 4)], start.at[:, pl.ds(4 * turn, 4)],
            s_recv.at[turn],
        )

    def start_out(turn):
        rows = pl.ds(4 * (BLOCKS - 1 - turn), 4)
        return pltpu.make_async_remote_copy(
            sec.at[0, :, rows], start.at[:, rows], s_send.at[turn], s_recv.at[turn],
            device_id=partner, device_id_type=MESH,
        )

    def start_wait(turn):
        rows = start.at[:, pl.ds(4 * row_of(m, turn), 4)]
        pltpu.make_async_copy(rows, rows, s_recv.at[turn]).wait()

    def edge_copies(kinds):
        plan = [
            (adv.at[:, 0], xfirst, partner),
            (advx.at[:, XROWS - 1], xlast, partner),
            (csend, cgot, partner),
            (ysend.at[0, 0], yhi, (0, gx, down)),
            (ysend.at[0, 1], yhi, (1, gx, down)),
            (ysend.at[1, 0], ylo, (0, gx, up)),
            (ysend.at[1, 1], ylo, (1, gx, up)),
            (xfirst, xhi, (1, left, gy)),
            (xlast, xlo, (0, right, gy)),
        ]
        for block in range(BLOCKS):
            rows = pl.ds(4 * block, 4)
            plan.append((advx.at[:, rows], adv.at[:, rows], partner))
        return [
            pltpu.make_async_remote_copy(
                plan[k][0], plan[k][1], e_send.at[k], e_recv.at[k],
                device_id=plan[k][2], device_id_type=MESH,
            )
            for k in kinds
        ]

    def corner_copies(sides=(0, 1)):
        return [
            pltpu.make_async_remote_copy(
                cgot.at[2 * xs + ys], (chi, clo)[xs].at[1 - ys], c_send.at[2 * xs + ys],
                c_recv.at[2 * xs + ys],
                device_id=(1 - xs, (left, right)[xs], (down, up)[ys]), device_id_type=MESH,
            )
            for xs in sides for ys in range(2)
        ]

    def plane_copy(j, arriving):
        _, tx, ty = plane_peer(j)
        to = (tx % CX) * CY + ty
        me = x * CY + gy
        if arriving:
            me = ((x + CX - j // CY) % CX) * CY + (gy + CY - j % CY) % CY
        return pltpu.make_async_remote_copy(
            fa.at[pl.ds(pl.multiple_of(to * 8, 8), 8)],
            fb1.at[pl.ds(pl.multiple_of(me * 8, 8), 8)],
            f_send.at[0, j], f_recv.at[0, j], device_id=plane_peer(j), device_id_type=MESH,
        )

    def line_copy(j, arriving=False):
        to, me = (z + j) % CZ, z
        if arriving:
            me = (z + CZ - j) % CZ
        return pltpu.make_async_remote_copy(
            fs2.at[pl.ds(pl.multiple_of(to * 16, 16), 16)],
            fb2.at[pl.ds(pl.multiple_of(me * 16, 16), 16)],
            f_send.at[1, j], f_recv.at[1, j], device_id=line_peer(j), device_id_type=MESH,
        )

    def table_copy():
        return pltpu.make_async_remote_copy(
            fb2, fb2, f_send.at[1, 0], f_recv.at[1, 0], device_id=partner, device_id_type=MESH
        )

    @pl.when(m == 0)
    def _():
        small[1].start()
        for block in ROWS:
            current_in(block).start()
        greet([partner, (0, gx, down), (0, gx, up)])
        greet([(1, left, gy), (1, left, down), (1, left, up)])
        for k, copy in enumerate(small):
            if k != 1:
                copy.start()
        small[1].wait()

        def put(p, row, value, raw):
            for k in range(2):
                part = value[:, k * LEV:(k + 1) * LEV]
                f = 2 * p + k
                if row < XROWS:
                    adv[f, row] = part.astype(bf16)
                else:
                    advx[f, row - XROWS] = part.astype(bf16)
                for side, edge in ((0, 0), (1, YROWS - 1)):
                    line = part[edge:edge + 1, :]
                    yrow[side, f, row:row + 1, :] = line
                    if raw is not None:
                        csend[2 * raw + side, f:f + 1, :] = line

        for turn, block in enumerate(ROWS):
            current_in(block).wait()
            for k in range(2):
                wind[k, block] = cur[k, 4 * block:4 * block + 4].reshape(NODES, LEV).astype(f32)
            for p in range(PAIRS):
                pair = [
                    cur[2 * p + k, 4 * block:4 * block + 4].reshape(NODES, LEV) for k in range(2)
                ]
                once = jnp.concatenate(pair, axis=1)
                slopes = mm(derive[...], jnp.concatenate([once, once], axis=0))
                u, v = wind[0, block], wind[1, block]
                value = jnp.concatenate([u, u], axis=1) * slopes[:NODES]
                value = value + jnp.concatenate([v, v], axis=1) * slopes[NODES:]
                first, last = value[:YROWS], value[3 * YROWS:]
                if block == 0:
                    put(p, 0, first, 0)
                elif block == 2 * BLOCKS - 1:
                    raw_first[p] = first
                    put(p, 4 * block + 3, last, 1)
                else:
                    shared = raw_last[p] + first
                    put(p, 4 * block - 1, shared, None)
                    put(p, 4 * block, shared, None)
                put(p, 4 * block + 1, value[YROWS:2 * YROWS], None)
                put(p, 4 * block + 2, value[2 * YROWS:3 * YROWS], None)
                if block == 2 * BLOCKS - 2:
                    shared = last + raw_first[p]
                    put(p, 4 * block + 3, shared, None)
                    put(p, 4 * block + 4, shared, None)
                elif block < 2 * BLOCKS - 2:
                    raw_last[p] = last
            if turn == 1:
                pl.semaphore_wait(barrier, 5)
                for copy in edge_copies((0, 1, 2)):
                    copy.start()
        for f in range(NF):
            for side in range(2):
                for half in range(2):
                    lines = yrow[side, f, half * XROWS:(half + 1) * XROWS]
                    ysend[side, half, f] = lines.astype(bf16)
        for copy in edge_copies((3, 4, 5, 6, 9, 10, 11, 12)):
            copy.start()
        xhi[...] = jnp.zeros_like(xhi)
        chi[...] = jnp.zeros_like(chi)

    @pl.when(m == 1)
    def _():
        small[0].start()
        greet([plane_peer(j) for j in PLANE])
        greet([line_peer(j) for j in LINE])
        greet([(1, right, gy), (1, right, down), (1, right, up)])
        greet([partner, (0, gx, down), (0, gx, up)])
        for turn in range(BLOCKS):
            start_in(turn).start()
        for copy in small[1:]:
            copy.start()
        small[0].wait()
        for g in range(NTEND):
            f2[4 * g:4 * g + 4, :] = frc_v[g]
        source = iota((128, 256), 0)
        source = 2 * ((source % CZ) * (CX * CY) + source // CZ)
        slot = iota((128, 256), 1)
        rows_high, rows_low = halves(f2[...])
        empty = jnp.zeros((32, 256), bf16)
        total = jnp.zeros((128, 128), f32)
        for r in range(2):
            pick = (slot == source + r).astype(f32).astype(bf16)
            for part in (rows_high, rows_low):
                stack = [empty] * 4
                stack[r] = part
                total = total + mm_nt(pick, jnp.concatenate(stack, axis=0))
        fa[...] = total
        xlo[...] = jnp.zeros_like(xlo)
        clo[...] = jnp.zeros_like(clo)
        pl.semaphore_wait(barrier, 29)
        for j in PLANE:
            plane_copy(j, False).start()
        for turn in range(BLOCKS):
            start_out(turn).start()
        for copy in edge_copies((0, 1, 2)):
            copy.wait_recv()
        for copy in edge_copies((7, 8)) + corner_copies():
            copy.start()
        mine = pl.ds(pl.multiple_of((x * CY + gy) * 8, 8), 8)
        fb1[mine, :] = fa[mine, :]

    def relay():
        for j in range(1, CX * CY):
            plane_copy(j, True).wait_recv()
        for k in range(CZ):
            fs2[16 * k:16 * k + 16, :] = fb1[pl.ds(k, 16, stride=CZ), :]
        for j in LINE:
            line_copy(j).start()
        mine = pl.ds(pl.multiple_of(z * 16, 16), 16)
        fb2[mine, :] = fs2[mine, :]

    for copy in small[3:]:
        copy.wait()
    spread = (iota((16, 128), 0) == (iota((16, 128), 1) // 32) * 4 + iota((16, 128), 1) % 4)
    spread = spread.astype(f32).astype(bf16)
    inside = (iota((128, 128), 0) // 4) % 8 == (iota((128, 128), 1) // 4) % 8
    for k in range(3):
        for block in range(BLOCKS):
            for ey in range(8):
                row = block * 32 + ey * 4
                one = tc_v[block, ey] if k == 0 else tn_v[block + BLOCKS * (k - 1), ey]
                ts[row:row + 4, :] = one.astype(f32)
        wide = jnp.where(inside, mm(ts[...].astype(bf16), spread), 0.0)
        if k == 0:
            for block in range(BLOCKS):
                win[block] = wide[32 * block:32 * block + 32].astype(bf16)
        else:
            turned = jnp.transpose(wide * DT_PHY)
            for block in range(BLOCKS):
                moved = turned if block == 0 else pltpu.roll(turned, 128 - 32 * block, 1)
                wgiven[block + BLOCKS * (k - 1)] = moved.astype(bf16)
    v_high, v_low = halves(v_v[...])
    vv[0:128, 0:128] = v_high
    vv[128:256, 0:128] = v_high
    vv[0:128, 128:256] = v_low
    vv[128:256, 128:256] = jnp.zeros((128, 128), bf16)

    owned = (iota((128, 64), 0) == own_v[...]).astype(f32)
    before = (iota((64, 64), 0) < iota((64, 64), 1)).astype(f32).astype(bf16)
    rank = mm(owned.astype(bf16), before)
    mine = (iota((256, 64), 1) == iota((256, 64), 0) // 4).astype(f32).astype(bf16)
    from0 = mm_nt(mine, jnp.where(rank < 0.5, owned, 0.0).astype(bf16)).astype(bf16)
    from1 = mm_nt(mine, jnp.where(rank < 0.5, 0.0, owned).astype(bf16)).astype(bf16)

    for g in range(NTEND):
        k, lane = iota((128, LEV), 0), iota((128, LEV), 1)
        chosen[g] = ((k % 32 // 4 == g) & (k // 64 == lane // 64)).astype(f32).astype(bf16)

    @pl.when(m == 0)
    def _():
        small[2].wait()
        small[0].wait()
        for copy in edge_copies((3, 5)):
            copy.wait_recv()

    @pl.when(m == 1)
    def _():
        small[1].wait()
        small[2].wait()
        relay()
        for copy in edge_copies((4, 6)):
            copy.wait_recv()

    lower = iota((YROWS, LEV), 1) < LEV // 2

    def pack(block, f, value):
        for i in range(2):
            a = value[i * YROWS:(i + 1) * YROWS]
            b = value[(i + 2) * YROWS:(i + 3) * YROWS]
            packed[0, block, f, i] = jnp.where(lower, a, pltpu.roll(b, 64, 1)).astype(bf16)
            packed[1, block, f, i] = jnp.where(lower, pltpu.roll(a, 64, 1), b).astype(bf16)

    def out_copy(turn, arriving=False):
        row = row_of(m, turn)
        return pltpu.make_async_remote_copy(
            packed.at[other, row], landed.at[row_of(other, turn) if arriving else row],
            o_send.at[turn], o_recv.at[turn], device_id=partner, device_id_type=MESH,
        )

    at = iota((XROWS, LEV), 0)

    for turn in range(BLOCKS):
        row = row_of(m, turn)
        final = turn == BLOCKS - 1
        start_wait(turn)

        @pl.when(m == 0)
        def _():
            if final:
                for copy in edge_copies((8,)) + corner_copies((1,)):
                    copy.wait_recv()

        @pl.when(m == 1)
        def _():
            edge_copies((9 + turn,))[0].wait_recv()
            if final:
                for copy in edge_copies((7,)) + corner_copies((0,)):
                    copy.wait_recv()

        weights = win[row]
        for p in range(PAIRS):
            parts, begun = [], []
            for k in range(2):
                f = 2 * p + k
                rows = [adv[f, 4 * row + i] for i in range(4)]
                halo = [ylo[f], yhi[f]]
                if final:
                    rows[0] = (rows[0].astype(f32) + xlo[f].astype(f32)).astype(bf16)
                    rows[3] = (rows[3].astype(f32) + xhi[f].astype(f32)).astype(bf16)
                    for side in range(2):
                        first = jnp.broadcast_to(clo[side, f:f + 1, :], (XROWS, LEV))
                        ending = jnp.broadcast_to(chi[side, f:f + 1, :], (XROWS, LEV))
                        extra = jnp.where(at == 0, first, jnp.where(at == XROWS - 1, ending, 0.0))
                        halo[side] = (halo[side].astype(f32) + extra).astype(bf16)
                parts.append(jnp.concatenate(rows + halo, axis=0))
                begun.append(start[f, pl.ds(4 * row, 4)].reshape(NODES, LEV).astype(f32))
            value = mm(advance[row], jnp.concatenate(parts, axis=1))
            value = (value + jnp.concatenate(begun, axis=1)).astype(bf16)
            got = mm(weights, value)
            for k in range(2):
                f = 2 * p + k
                advd[f, turn] = value[:, k * LEV:(k + 1) * LEV]
                one = got[:, k * LEV:(k + 1) * LEV]
                cells[turn, f] = one
                high, low = halves(one)
                split[turn, f, :, 0:LEV] = high
                split[turn, f, :, LEV:2 * LEV] = low
        got = mm(split[turn].reshape(NF * CELLS, 2 * LEV), vv[...])
        got = got[:, :LEV] + got[:, LEV:]
        warm = jnp.tanh(got)
        for f in range(NF):
            mixed[turn, f] = got[f * CELLS:(f + 1) * CELLS]
            act[turn, f] = warm[f * CELLS:(f + 1) * CELLS]
        for g in range(NTEND):
            acc = rel_v[g:g + 1, :] * (mixed[turn, g] - cells[turn, g])
            for f in range(NF):
                acc = acc + cpl_v[g, f] * act[turn, f]
            tend[turn, g] = acc.astype(bf16)
        for f in range(NTEND, NF):
            pack(row, f, advd[f, turn].astype(f32))
        weights = wgiven[m * BLOCKS + row][:, 0:CELLS]
        for p in range(NTEND // 2):
            pair = (2 * p, 2 * p + 1)
            value = mm(weights, jnp.concatenate([tend[turn, f] for f in pair], axis=1))
            for k, f in enumerate(pair):
                pack(row, f, value[:, k * LEV:(k + 1) * LEV] + advd[f, turn].astype(f32))
        out_copy(turn).start()

    @pl.when(m == 0)
    def _():
        for copy in edge_copies((0, 1, 2, 3, 4, 5, 6, 9, 10, 11, 12)):
            copy.wait_send()

    @pl.when(m == 1)
    def _():
        for turn in range(BLOCKS):
            start_out(turn).wait_send()
        for copy in edge_copies((7, 8)) + corner_copies():
            copy.wait_send()
        for j in range(1, CX * CY):
            plane_copy(j, False).wait_send()
        for j in range(1, CZ):
            line_copy(j).wait_send()

    @pl.when(m == 0)
    def _():
        table_copy().wait_recv()

    @pl.when(m == 1)
    def _():
        for j in range(1, CZ):
            line_copy(j, True).wait_recv()
        table_copy().start()

    table = fb2[...]
    lines = mm2(from0, table) + mm2(from1, pltpu.roll(table, 96, 1))
    lane = iota((256, 128), 1)
    lines = jnp.where((lane < 32) & (lane % 4 == iota((256, 128), 0) % 4), lines, 0.0)
    lines = lines + pltpu.roll(lines, 32, 1)
    lines = lines + pltpu.roll(lines, 64, 1)
    quarter = iota((2 * YROWS, LEV), 1) // 32
    for block in range(2 * BLOCKS):
        got = mm2(wgiven[block, :, 0:32], lines[32 * block:32 * block + 32])
        both = jnp.where(quarter < 2, got[:2 * YROWS], got[2 * YROWS:])
        high = both.astype(bf16).astype(f32)
        given[block] = jnp.where(quarter % 2 == 0, high, both - high).astype(bf16)

    @pl.when(m == 1)
    def _():
        table_copy().wait_send()

    for turn in range(BLOCKS):
        out_copy(turn).wait_send()
        out_copy(turn, True).wait_recv()


ROWS = (7, 0, 1, 2, 3, 4, 5, 6)


def hops_to(j, count):
    return min(j % count, count - j % count)


PLANE = sorted(range(1, CX * CY), key=lambda j: -hops_to(j // CY, CX) - hops_to(j, CY))
LINE = sorted(range(1, CZ), key=lambda j: -hops_to(j, CZ))


def main_call(args):
    v = pltpu.VMEM
    packed_shape = (BLOCKS, NF, 2, YROWS, LEV)
    dma = pltpu.SemaphoreType.DMA
    scratch = [
        v((NF, 2 * XROWS, YROWS, LEV), bf16),
        v((NF, XROWS, YROWS, LEV), bf16),
        v((NF, XROWS, YROWS, LEV), bf16),
        v((NF, XROWS, YROWS, LEV), bf16),
        v((NF, BLOCKS, NODES, LEV), bf16),
        v((2, 2 * BLOCKS, NODES, LEV), f32),
        v((NF, YROWS, LEV), bf16),
        v((NF, YROWS, LEV), bf16),
        v((NF, YROWS, LEV), bf16),
        v((NF, YROWS, LEV), bf16),
        v((2, NF, 2 * XROWS, LEV), f32),
        v((2, 2, NF, XROWS, LEV), bf16),
        v((NF, XROWS, LEV), bf16),
        v((NF, XROWS, LEV), bf16),
        v((4, 16, LEV), f32),
        v((4, 16, LEV), f32),
        v((2, 16, LEV), f32),
        v((2, 16, LEV), f32),
        v((PAIRS, YROWS, 2 * LEV), f32),
        v((PAIRS, YROWS, 2 * LEV), f32),
        v((BLOCKS, 8, 4, 16), bf16),
        v((2 * BLOCKS, 8, 4, 16), bf16),
        v((1, 64), jnp.int32),
        v((NTEND, 4, 256), f32),
        v((LEV, LEV), f32),
        v((NTEND, LEV), f32),
        pltpu.SMEM((NTEND, NF), f32),
        v((2 * NODES, 2 * NODES), bf16),
        v((BLOCKS, NODES, NODES + 2 * XROWS), bf16),
        v((32, 256), f32),
        v((128, 16), f32),
        v((BLOCKS, CELLS, 128), bf16),
        v((2 * BLOCKS, 128, 128), bf16),
        v((256, 256), bf16),
    ]
    scratch += [v((128, 128), f32)] * 4
    scratch += [
        v((BLOCKS, NF, CELLS, LEV), f32),
        v((BLOCKS, NF, CELLS, 2 * LEV), bf16),
        v((BLOCKS, NF, CELLS, LEV), f32),
        v((BLOCKS, NF, CELLS, LEV), f32),
        v((BLOCKS, NTEND, CELLS, LEV), bf16),
        dma((9,)), dma((2 * BLOCKS,)), dma((BLOCKS,)), dma((BLOCKS,)),
        dma((9 + BLOCKS,)), dma((9 + BLOCKS,)), dma((4,)), dma((4,)),
        dma((2, CX * CY)), dma((2, CX * CY)), dma((BLOCKS,)), dma((BLOCKS,)),
    ]
    return pl.pallas_call(
        main_kernel,
        out_shape=(
            jax.ShapeDtypeStruct((2,) + packed_shape, bf16),
            jax.ShapeDtypeStruct(packed_shape, bf16),
            jax.ShapeDtypeStruct((2 * BLOCKS, 2 * YROWS, LEV), bf16),
            jax.ShapeDtypeStruct((NTEND, 128, LEV), bf16),
        ),
        in_specs=[HBM] * 10,
        out_specs=(VMEM,) * 4,
        scratch_shapes=scratch,
        compiler_params=pltpu.CompilerParams(
            collective_id=0, has_side_effects=True, vmem_limit_bytes=40 * 2**20
        ),
    )(*args)


def unpack_kernel(packed, landed, given, chosen, out, stage, sems):
    m = lax.axis_index("grp")

    def copy(k, block):
        rows = (m if k == 0 else 1 - m) * XROWS + 4 * block
        return pltpu.make_async_copy(
            stage.at[k, block], out.at[:, pl.ds(rows, 4)], sems.at[k, block]
        )

    for k in range(2):
        for block in range(BLOCKS):
            lines = given[(m if k == 0 else 1 - m) * BLOCKS + block]
            for f in range(NF):
                if f < NTEND:
                    added = mm(lines, chosen[f])
                for i in range(2):
                    line = packed[m, block, f, i] if k == 0 else landed[block, f, i]
                    line = line.astype(f32)
                    if f < NTEND:
                        line = line + added[i * YROWS:(i + 1) * YROWS]
                    stage[k, block, f, i] = line[:, :LEV // 2].astype(bf16)
                    moved = pltpu.roll(line, 64, 1)
                    stage[k, block, f, i + 2] = moved[:, :LEV // 2].astype(bf16)
            copy(k, block).start()
    for k in range(2):
        for block in range(BLOCKS):
            copy(k, block).wait()


def unpack_call(*arrays):
    return pl.pallas_call(
        unpack_kernel,
        out_shape=jax.ShapeDtypeStruct((NF, 2 * XROWS, YROWS, LEV // 2), bf16),
        in_specs=[VMEM] * 4,
        out_specs=HBM,
        scratch_shapes=[
            pltpu.VMEM((2, BLOCKS, NF, 4, YROWS, LEV // 2), bf16),
            pltpu.SemaphoreType.DMA((2, BLOCKS)),
        ],
        compiler_params=pltpu.CompilerParams(vmem_limit_bytes=24 * 2**20),
    )(*arrays)


def shards(
    section_levels, to_cells, to_nodes, owner_map, forcing, vertical_map, coupling, relaxation
):
    derive, advance = (jnp.asarray(c) for c in constants())
    operands = (
        section_levels, to_cells, jnp.swapaxes(to_nodes, 2, 3), owner_map.reshape(1, 64),
        forcing[0, 0], vertical_map, coupling, relaxation, derive, advance,
    )
    results = main_call([
        pltpu.with_memory_space_constraint(x, pltpu.HBM) for x in operands
    ])
    return unpack_call(*results)


def solution(mesh):
    in_specs = (
        P("grp", None, "gx", "gy", None),
        P("gx", "gy", None, None),
        P("gx", "gy", None, None),
        P("gx", "gy", None, None),
        P("gx", "gy", None, None, None),
        P(),
        P(),
        P(),
    )
    out_specs = P(None, "gx", "gy", "grp")
    return jax.shard_map(shards, mesh=mesh, in_specs=in_specs, out_specs=out_specs, check_vma=False)
```
